256 devices in a mesh: rep: 4 (over x), ep: 64 (over z, y, core).
Axes of the slice: x: 4, y: 4, z: 8, core: 2. Of those that a mesh axis runs over, the one named last changes fastest.
Arguments:
- out_grad: bfloat16 [4096, 128, 256], P(('rep', 'ep')), may hold values from -3 to 3
- routes: int32 [4096, 2], P(('rep', 'ep')), may hold values from 0 to 63, all different within a row; in each aligned block of 16 rows (0 to 15, 16 to 31, ...) at most 2 rows name the same one
- gates: bfloat16 [4096, 2], P(('rep', 'ep')), may hold values from 0.19921875 to 1
- stash: bfloat16 [4, 64, 64, 2, 128, 256], P('rep', 'ep'), may hold values from -6 to 6
- weights: bfloat16 [64, 9, 4, 32, 32], P('ep'), may hold values from -0.375 to 0.375
Outputs:
- in_grad: bfloat16 [4096, 128, 256], P(('rep', 'ep'))
- weight_grad: float32 [64, 9, 4, 32, 32], P('ep')
The draws below stay inside these ranges and needn't reach their ends.
Inputs may be any that keep to these rules, and one draw needn't show every extreme that they name: Among the routes of the patches of one device, at most 2 name one expert, and some device reaches 2; the 2 experts of a patch differ.
All inputs are finite; a program needn't handle non-finite values.
Results may differ from the reference program's by a relative error of at most 0.014.
Values may be sent and summed in bfloat16 or wider, within the bound.
No kernel may reach another device: no remote copies, remote signals or barrier semaphores. Data moves between devices by JAX's collectives and lax.ppermute only.
A program may use at most 192 MiB of HBM per device.

```python
import math
import jax
import jax.numpy as jnp
import numpy as np
from jax import lax

C = 128
GROUP = 32
SIDE = 16
TOP = 2
TOK_DEV = 16
GROUPS = 4
POSITIONS = 256
EXPERTS = 64
CAP = 2
REPS = 4
SOURCES = 64
TOKENS = 4096
N_REP = 4
N_EP = 64


def block_levels(rng, shape, shards, low, high):
    def one(axis_at, shards_of):
        draws = jax.random.uniform(jax.random.fold_in(jax.random.fold_in(rng, 6), axis_at), (shards_of,), jnp.float32, low / len(shards), high / len(shards))
        return jnp.repeat(jnp.exp(draws), shape[axis_at] // shards_of).reshape((-1,) + (1,) * (len(shape) - axis_at - 1))

    gain = one(*shards[0])
    for cut in shards[1:]:
        gain = gain * one(*cut)
    return gain


def assign_block(rng, own, number, rows, number_of, top, limit, skew):
    order = jax.random.permutation(rng, number_of)
    crowded, common = shares(number_of, rows * top, limit, skew, True), shares(number_of, rows * top, limit, skew, False)
    places = jnp.arange(number_of)

    def named(tallies, turn):
        used = int((tallies > 0).sum())
        fixed = max(1, used // 4)
        shifted = fixed + (places - fixed + turn * (used - fixed)) % max(1, number_of - fixed)
        return jnp.zeros((number_of,), jnp.int32).at[order[jnp.where(places < fixed, places, shifted)]].set(jnp.asarray(tallies, jnp.int32))

    tallies = jnp.where(number % 4 == 0, named(crowded, number // 4), named(common, number - number // 4 - 1))
    mixed = jax.random.permutation(jax.random.fold_in(own, 3), number_of)
    source_of, receiver = mixed[0:number_of // 2 * 2:2], mixed[1:number_of // 2 * 2:2]
    room = jnp.minimum(tallies[source_of] - 1, limit - tallies[receiver]) // 2
    room = jnp.where((source_of == order[0]) | (receiver == order[0]) | (tallies[receiver] == 0), 0, jnp.maximum(room, 0))
    shifted = jax.random.randint(jax.random.fold_in(own, 4), (number_of // 2,), 0, 1 << 20) % (room + 1)
    tallies = tallies.at[source_of].add(-shifted).at[receiver].add(shifted)
    items = jnp.searchsorted(jnp.cumsum(tallies), jnp.arange(rows * top), side="right").astype(jnp.int32)
    table = items.reshape(top, rows).T
    table = table[jax.random.permutation(jax.random.fold_in(own, 1), rows)]
    turn = jax.random.randint(jax.random.fold_in(own, 2), (rows, 1), 0, top)
    return jnp.take_along_axis(table, (jnp.arange(top)[None, :] + turn) % top, axis=1)


def shares(number_of, total, most, slope, full):
    portions = [(1 << 20) // math.isqrt(grade ** slope) + 1 for grade in range(1, number_of + 1)]
    largest = most if full else min(most, max(-(-total // number_of), total * portions[0] // sum(portions)))
    least = 1 if total - largest >= number_of - 1 else 0
    counts, surplus = [largest] + [least] * (number_of - 1), total - largest - least * (number_of - 1)
    while surplus > 0:
        free = [i for i in range(1, number_of) if counts[i] < largest] or [i for i in range(1, number_of) if counts[i] < most]
        mass, left = sum([portions[i] for i in free]), surplus
        for i in free:
            more = min(most - counts[i], max(1, left * portions[i] // mass), surplus)
            counts[i] = counts[i] + more
            surplus = surplus - more
    return np.array(counts)


def normal_values(stream_key, extent, scale, limit, pieces=(), kind=jnp.bfloat16):
    entries = jax.random.normal(stream_key, extent, jnp.float32) * scale
    if len(pieces) > 0:
        entries = block_levels(stream_key, extent, pieces, -0.22, 0.18) * entries
    return jnp.clip(entries, min=-limit, max=limit).astype(kind)


def setup_inputs(seed: int = 0) -> dict:
    key_of = jax.random.split(jax.random.key(seed), 6)
    out_grad = normal_values(key_of[0], (TOKENS, C, POSITIONS), 0.5, 3.0, ((0, 256),))
    routes_keys = jax.random.split(jax.random.fold_in(key_of[1], 1), TOKENS // TOK_DEV)
    routes_turns = jax.random.permutation(jax.random.fold_in(key_of[1], 3), TOKENS // TOK_DEV)
    routes = jax.vmap(lambda own, number: assign_block(jax.random.fold_in(key_of[1], 2), own, number, TOK_DEV, EXPERTS, TOP, CAP, 2))(routes_keys, routes_turns).reshape((TOKENS, TOP))
    gates = jnp.clip(0.19921875 + 0.80078125 * jax.random.uniform(key_of[2], (TOKENS, TOP), jnp.float32) ** block_levels(key_of[2], (TOKENS, TOP), ((0, 256),), -0.2, 0.2), 0.19921875, 1.0).astype(jnp.bfloat16)
    stash = normal_values(key_of[3], (REPS, EXPERTS, SOURCES, CAP, C, POSITIONS), 1.0, 6.0, ((0, 4), (1, 64)))
    weights = normal_values(key_of[4], (EXPERTS, 9, GROUPS, GROUP, GROUP), (9 * GROUP) ** -0.5, 0.375, ((0, 64),))
    return {"out_grad": out_grad, "routes": routes, "gates": gates, "stash": stash, "weights": weights}


tap_offsets = [(-1, -1), (-1, 0), (-1, 1), (0, -1), (0, 0), (0, 1), (1, -1), (1, 0), (1, 1)]

def shift_cells(values, row_step, col_step):
    position = jnp.arange(SIDE * SIDE, dtype=jnp.int32)
    cell_row = position // SIDE
    cell_col = position % SIDE
    inside = (cell_row + row_step >= 0) & (cell_row + row_step < SIDE) & (cell_col + col_step >= 0) & (cell_col + col_step < SIDE)
    rolled = jnp.roll(values, -(row_step * SIDE + col_step), axis=-1)
    return jnp.where(inside, rolled, jnp.zeros_like(rolled))

def slot_positions(route_row):
    onehot = (route_row[:, None] == jnp.arange(EXPERTS, dtype=jnp.int32)[None, :]).astype(jnp.int32)
    earlier = jnp.cumsum(onehot, 0) - onehot
    return lax.optimization_barrier(jnp.sum(earlier * onehot, 1)).astype(jnp.int32)

def route_input_grad(scaled, chosen):
    route_count = scaled.shape[0]
    grouped = scaled.reshape(route_count, GROUPS, GROUP, POSITIONS).astype(jnp.float32)
    summed = jnp.zeros((route_count, GROUPS, GROUP, POSITIONS), jnp.float32)
    for tap_index, (row_step, col_step) in enumerate(tap_offsets):
        mixed = jnp.einsum('rgdc,rgdp->rgcp', chosen[:, tap_index].astype(jnp.float32), grouped)
        summed = summed + shift_cells(mixed, -row_step, -col_step)
    return summed.reshape(route_count, C, POSITIONS).astype(jnp.bfloat16)

def reference(out_grad, routes, gates, stash, weights):
    device_count = N_REP * N_EP
    slot_index = jax.vmap(slot_positions)(routes.reshape(device_count, TOK_DEV * TOP)).reshape(-1)
    experts = routes.reshape(-1)
    scaled = (gates.astype(jnp.float32)[:, :, None, None] * out_grad.astype(jnp.float32)[:, None]).astype(jnp.bfloat16)
    scaled = scaled.reshape(TOKENS * TOP, C, POSITIONS)
    source = jnp.arange(TOKENS * TOP, dtype=jnp.int32) // (TOK_DEV * TOP)
    group_index = source // N_EP
    source_ep = source % N_EP
    dispatched = jnp.zeros((N_REP, EXPERTS, N_EP, CAP, C, POSITIONS), jnp.bfloat16)
    dispatched = dispatched.at[group_index, experts, source_ep, slot_index].set(scaled)

    def expert_grad(expert):
        grads_in = dispatched[:, expert].reshape(-1, GROUPS, GROUP, POSITIONS).astype(jnp.float32)
        inputs = stash[:, expert].reshape(-1, GROUPS, GROUP, POSITIONS).astype(jnp.float32)
        return jnp.stack([jnp.einsum('sgdp,sgcp->gdc', grads_in, shift_cells(inputs, row_step, col_step)) for row_step, col_step in tap_offsets])
    weight_grad = lax.map(expert_grad, jnp.arange(EXPERTS, dtype=jnp.int32))
    route_grad = route_input_grad(scaled, weights[experts])
    in_grad = lax.optimization_barrier(jnp.sum(route_grad.reshape(TOKENS, TOP, C, POSITIONS).astype(jnp.float32), 1)).astype(jnp.bfloat16)
    return (in_grad, weight_grad)
```

```python
import functools

import jax
import jax.numpy as jnp
from jax import lax
from jax.experimental import pallas as pl
from jax.experimental.pallas import tpu as pltpu
from jax.sharding import PartitionSpec as P

SIDE = 16
CELLS = 256
GROUPS = 4
WIDTH = 32
CHANNELS = 128
NZ, NY, NC, NX = 8, 4, 2, 4
PIECE = 80
DEPTH = 6


def ep_perm(dz, dy, dc):
    pairs = []
    for z in range(NZ):
        for y in range(NY):
            for c in range(NC):
                to = ((z + dz) % NZ, (y + dy) % NY, c ^ dc)
                pairs.append(((z * NY + y) * NC + c, (to[0] * NY + to[1]) * NC + to[2]))
    return pairs


def rep_perm(dx):
    return [(x, (x + dx) % NX) for x in range(NX)]


def shifted(values, row_step, col_step, cell):
    if row_step == 0 and col_step == 0:
        return values
    rolled = pltpu.roll(values, (-(row_step * SIDE + col_step)) % CELLS, 1)
    row, col = cell // SIDE + row_step, cell % SIDE + col_step
    inside = (row >= 0) & (row < SIDE) & (col >= 0) & (col < SIDE)
    return jnp.where(inside, rolled, 0.0)


def input_kernel(place_ref, gate_ref, grad_ref, weight_ref, out_ref, lhs_ref, rhs_ref, stage_ref):
    patch = pl.program_id(0)
    cell = lax.broadcasted_iota(jnp.int32, (1, CELLS), 1)
    lane_group = lax.broadcasted_iota(jnp.int32, (WIDTH, CHANNELS), 1) // WIDTH
    grad = grad_ref[0].astype(jnp.float32)
    for b in (-1, 0, 1):
        by_col = shifted(grad, 0, -b, cell)
        for a in (-1, 0, 1):
            tap = 3 * (a + 1) + (b + 1)
            rhs_ref[tap * CHANNELS : (tap + 1) * CHANNELS, :] = shifted(
                by_col, -a, 0, cell
            ).astype(jnp.bfloat16)
    for k in range(2):
        for quarter in range(NX):
            stage_ref[quarter * PIECE : (quarter + 1) * PIECE, :] = weight_ref[
                place_ref[(patch * 2 + k) * NX + quarter]
            ]
        for tap in range(9):
            kernel = stage_ref[tap * WIDTH : (tap + 1) * WIDTH, :]
            for group in range(GROUPS):
                row = k * CHANNELS + group * WIDTH
                lhs_ref[row : row + WIDTH, tap * CHANNELS : (tap + 1) * CHANNELS] = jnp.where(
                    lane_group == group, kernel, jnp.zeros_like(kernel)
                )
    both = jnp.dot(lhs_ref[...], rhs_ref[...], preferred_element_type=jnp.float32)
    total = (
        gate_ref[patch * 2] * both[:CHANNELS] + gate_ref[patch * 2 + 1] * both[CHANNELS:]
    )
    out_ref[0] = total.astype(jnp.bfloat16)


def input_grads(place, gate, grad, weight):
    count = grad.shape[0]
    return pl.pallas_call(
        input_kernel,
        out_shape=jax.ShapeDtypeStruct(grad.shape, jnp.bfloat16),
        grid=(count,),
        in_specs=[
            pl.BlockSpec(memory_space=pltpu.SMEM),
            pl.BlockSpec(memory_space=pltpu.SMEM),
            pl.BlockSpec((1, CHANNELS, CELLS), lambda i: (i, 0, 0)),
            pl.BlockSpec(memory_space=pltpu.VMEM),
        ],
        out_specs=pl.BlockSpec((1, CHANNELS, CELLS), lambda i: (i, 0, 0)),
        scratch_shapes=[
            pltpu.VMEM((2 * CHANNELS, 9 * CHANNELS), jnp.bfloat16),
            pltpu.VMEM((9 * CHANNELS, CELLS), jnp.bfloat16),
            pltpu.VMEM((NX * PIECE, CHANNELS), jnp.bfloat16),
        ],
        compiler_params=pltpu.CompilerParams(vmem_limit_bytes=24 << 20),
        cost_estimate=pl.CostEstimate(
            flops=1, bytes_accessed=1, transcendentals=0
        ),
    )(place, gate, grad, weight)


def weight_kernel(halves, chunks, continued, row_of, gate_of, *refs):
    grads, refs = refs[:halves], refs[halves:]
    stash, refs = refs[:chunks], refs[chunks:]
    if continued:
        begun, refs = refs[0], refs[1:]
    out_ref = refs[0]
    (list_grad, list_row, list_chunk, list_gate, ends, grad_buf, stash_buf, lhs, rhs, total, sems) = refs[1:]
    held = grads[0].shape[0]
    cell = lax.broadcasted_iota(jnp.int32, (1, CELLS), 1)

    filled = jnp.int32(0)
    for chunk in range(chunks):

        def note(slot, filled, chunk=chunk):
            row = row_of[chunk * 16 + slot]
            list_grad[filled] = jnp.maximum(row, 0)
            list_row[filled] = slot
            list_chunk[filled] = chunk
            list_gate[filled] = gate_of[chunk * 16 + slot]
            return filled + (row >= 0).astype(jnp.int32)

        filled = lax.fori_loop(0, 16, note, filled)
        list_grad[filled] = 0
        list_row[filled] = 0
        list_chunk[filled] = chunk
        list_gate[filled] = 0.0
        filled = filled + (filled & 1)
        ends[chunk] = filled // 2
    pairs = filled // 2

    def start(pair):
        for j in range(2):
            at = pair * 2 + j
            slot = (pair % DEPTH) * 2 + j
            row = list_grad[at]
            for half in range(halves):

                @pl.when((row >= half * held) & (row < (half + 1) * held))
                def _(half=half):
                    pltpu.make_async_copy(
                        grads[half].at[row - half * held], grad_buf.at[slot], sems.at[slot, 0]
                    ).start()

            for chunk in range(chunks):

                @pl.when(list_chunk[at] == chunk)
                def _(chunk=chunk):
                    pltpu.make_async_copy(
                        stash[chunk].at[list_row[at]], stash_buf.at[slot], sems.at[slot, 1]
                    ).start()

    def finish(pair):
        for j in range(2):
            slot = (pair % DEPTH) * 2 + j
            pltpu.make_async_copy(grads[0].at[0], grad_buf.at[slot], sems.at[slot, 0]).wait()
            pltpu.make_async_copy(stash[0].at[0], stash_buf.at[slot], sems.at[slot, 1]).wait()

    for pair in range(DEPTH):

        @pl.when(pair < pairs)
        def _(pair=pair):
            start(jnp.int32(pair))

    begin = jnp.int32(0)
    for chunk in range(chunks):
        total[...] = begun[chunk] if continued else jnp.zeros_like(total)

        def step(pair, carry):
            finish(pair)
            for j in range(2):
                slot = (pair % DEPTH) * 2 + j
                cells = slice(j * CELLS, (j + 1) * CELLS)
                grad = grad_buf[slot].astype(jnp.float32) * list_gate[pair * 2 + j]
                kept = stash_buf[slot].astype(jnp.float32)
                for i, step_by in enumerate((-1, 0, 1)):
                    left = shifted(grad, -step_by, 0, cell).astype(jnp.bfloat16)
                    right = shifted(kept, 0, step_by, cell).astype(jnp.bfloat16)
                    for group in range(GROUPS):
                        rows = slice(group * WIDTH, (group + 1) * WIDTH)
                        lhs[group, i * WIDTH : (i + 1) * WIDTH, cells] = left[rows]
                        rhs[group, i * WIDTH : (i + 1) * WIDTH, cells] = right[rows]
            for group in range(GROUPS):
                total[group] += lax.dot_general(
                    lhs[group],
                    rhs[group],
                    (((1,), (1,)), ((), ())),
                    preferred_element_type=jnp.float32,
                )

            @pl.when(pair + DEPTH < pairs)
            def _():
                start(pair + DEPTH)

            return carry

        lax.fori_loop(begin, ends[chunk], step, 0)
        begin = ends[chunk]
        out_ref[chunk] = total[...].astype(out_ref.dtype)


def weight_grads(row_of, gate_of, grads, stash, begun, dtype):
    chunks, halves, continued = len(stash), len(grads), begun is not None
    place = pl.BlockSpec(memory_space=pl.ANY)
    extra = [begun] if continued else []
    return pl.pallas_call(
        functools.partial(weight_kernel, halves, chunks, continued),
        out_shape=jax.ShapeDtypeStruct((chunks, GROUPS, 3 * WIDTH, 3 * WIDTH), dtype),
        in_specs=[pl.BlockSpec(memory_space=pltpu.SMEM)] * 2
        + [place] * (halves + chunks)
        + [pl.BlockSpec(memory_space=pltpu.VMEM)] * len(extra),
        out_specs=pl.BlockSpec(memory_space=pltpu.VMEM),
        scratch_shapes=[
            pltpu.SMEM((18 * chunks,), jnp.int32),
            pltpu.SMEM((18 * chunks,), jnp.int32),
            pltpu.SMEM((18 * chunks,), jnp.int32),
            pltpu.SMEM((18 * chunks,), jnp.float32),
            pltpu.SMEM((chunks,), jnp.int32),
            pltpu.VMEM((2 * DEPTH, CHANNELS, CELLS), jnp.bfloat16),
            pltpu.VMEM((2 * DEPTH, CHANNELS, CELLS), jnp.bfloat16),
            pltpu.VMEM((GROUPS, 3 * WIDTH, 2 * CELLS), jnp.bfloat16),
            pltpu.VMEM((GROUPS, 3 * WIDTH, 2 * CELLS), jnp.bfloat16),
            pltpu.VMEM((GROUPS, 3 * WIDTH, 3 * WIDTH), jnp.float32),
            pltpu.SemaphoreType.DMA((2 * DEPTH, 2)),
        ],
        compiler_params=pltpu.CompilerParams(vmem_limit_bytes=56 << 20),
        cost_estimate=pl.CostEstimate(
            flops=1, bytes_accessed=1, transcendentals=0
        ),
    )(row_of.reshape(-1), gate_of.reshape(-1), *grads, *stash, *extra)


def stack_of(first, others):
    return jnp.concatenate([first[None]] + [o[None] for o in others], 0)


def per_device(out_grad, routes, gates, stash, weights):
    x, e = lax.axis_index("rep"), lax.axis_index("ep")
    z, y, c = e // (NY * NC), e // NC % NY, e % NC
    rows, top = routes.shape
    groups = [[zz * NY * NC + r for zz in range(NZ)] for r in range(NY * NC)]
    grads = lax.all_gather(out_grad, "ep", axis=0, tiled=True, axis_index_groups=groups)

    kept = stash.reshape(NZ, NY, NC, 2, CHANNELS, CELLS)
    offsets = [(0, 0), (0, 1), (1, 0), (3, 0), (1, 1), (3, 1), (2, 0), (2, 1)]

    def sent(kept, d, dc):
        part = lax.dynamic_slice(
            kept, (0, (y + d) % NY, c ^ dc, 0, 0, 0), (NZ, 1, 1, 2, CHANNELS, CELLS)
        )
        return part.reshape(NZ * 2, CHANNELS, CELLS)

    first = [sent(kept, d, dc) for d, dc in offsets[2:4]]
    mixed = weights[0].transpose(0, 3, 1, 2).reshape(9 * WIDTH, CHANNELS)
    mixed = jnp.pad(mixed, ((0, NX * PIECE - 9 * WIDTH), (0, 0)))
    piece = lax.dynamic_slice_in_dim(mixed, x * PIECE, PIECE, 0)
    note = jnp.concatenate(
        [routes.reshape(1, -1).astype(jnp.bfloat16), gates.reshape(1, -1)], 1
    )
    note = jnp.pad(note, ((0, 15), (0, CHANNELS - 2 * rows * top)))
    held = jnp.concatenate([piece, note], 0)
    kept, held, *first = lax.optimization_barrier((kept, held, *first))
    own, *rest = [sent(kept, d, dc) for d, dc in offsets[:2] + offsets[4:]]
    experts = [e - y * NC - c + ((y - d) % NY) * NC + (c ^ dc) for d, dc in offsets]
    experts = jnp.stack(experts)

    up = down = held
    from_z = {0: held}
    for d in range(1, NZ // 2 + 1):
        up = lax.ppermute(up, "ep", ep_perm(1, 0, 0))
        from_z[d] = up
        if d < NZ // 2:
            down = lax.ppermute(down, "ep", ep_perm(-1, 0, 0))
            from_z[NZ - d] = down
    held = jnp.stack([from_z[d] for d in range(NZ)])
    notes = held[:, PIECE, : 2 * rows * top].astype(jnp.float32)
    held = held[:, :PIECE]
    held, *rest = lax.optimization_barrier((held, *rest))
    rest = rest[:1] + first + rest[1:]
    chunks = [own] + [
        lax.ppermute(part, "ep", ep_perm(0, d, dc)) for part, (d, dc) in zip(rest, offsets[1:])
    ]
    held = stack_of(held, [lax.ppermute(held, "ep", ep_perm(0, d, 0)) for d in range(1, NY)])
    held = held.reshape(NY * NZ, PIECE, CHANNELS)
    held, chunks[2], chunks[3] = lax.optimization_barrier((held, chunks[2], chunks[3]))
    held = stack_of(held, [lax.ppermute(held, "rep", rep_perm(d)) for d in range(1, NX)])
    held, chunks[4], chunks[5] = lax.optimization_barrier((held, chunks[4], chunks[5]))
    held = stack_of(held, [lax.ppermute(held, "ep", ep_perm(0, 0, 1))])
    held = held.reshape(NC * NX * NY * NZ, PIECE, CHANNELS)

    from_z = (z - jnp.arange(NZ, dtype=jnp.int32)) % NZ
    notes = jnp.sum(
        jnp.where((from_z[:, None] == jnp.arange(NZ)[None])[:, :, None], notes[:, None], 0.0), 0
    )
    named = notes[:, : rows * top].astype(jnp.int32)
    gate = notes[:, rows * top :]
    here = experts[:, None, None] == named[None]
    order = jnp.arange(rows * top, dtype=jnp.int32)
    before = (order[:, None] < order[None, :])[None, None] & here[:, :, :, None]
    earlier = jnp.sum(before.astype(jnp.int32), 2)
    chosen = here[:, :, None, :] & (earlier[:, :, None, :] == jnp.arange(2)[None, None, :, None])
    source_row = jnp.arange(NZ, dtype=jnp.int32)[:, None] * rows + (order // top)[None]
    row_of = jnp.max(jnp.where(chosen, source_row[None, :, None, :], -1), 3)
    gate_of = jnp.sum(jnp.where(chosen, gate[None, :, None, :], 0.0), 3)
    flat = routes.reshape(-1)
    at_z, at_y, at_c = flat // (NY * NC), flat // NC % NY, flat % NC
    block = ((y - at_y) % NY) * NZ + (z - at_z) % NZ
    quarter = (x - jnp.arange(NX, dtype=jnp.int32)) % NX
    place = ((at_c ^ c)[:, None] * NX + quarter[None]) * (NZ * NY) + block[:, None]
    in_grad = input_grads(
        place.reshape(-1), gates.reshape(-1).astype(jnp.float32), out_grad, held
    )

    in_grad, row_of = lax.optimization_barrier((in_grad, row_of))
    early = weight_grads(row_of[:6], gate_of[:6], [grads], chunks[:6], None, jnp.bfloat16)
    late = weight_grads(row_of[6:], gate_of[6:], [grads], chunks[6:], None, jnp.bfloat16)
    parts = [early[i] for i in range(6)] + [late[i] for i in range(2)]

    total = None
    for part, (d, dc) in zip(parts, offsets):
        if d or dc:
            part = lax.ppermute(part, "ep", ep_perm(0, -d, dc))
        part = part.astype(jnp.float32)
        total = part if total is None else total + part
    total = total.astype(jnp.bfloat16)
    summed = total.astype(jnp.float32)
    for d in range(1, NX):
        summed = summed + lax.ppermute(total, "rep", rep_perm(d)).astype(jnp.float32)
    weight_grad = summed.reshape(GROUPS, 3, WIDTH, 3, WIDTH).transpose(1, 3, 0, 2, 4)
    return in_grad, weight_grad.reshape(1, 9, GROUPS, WIDTH, WIDTH)


def solution(mesh):
    return jax.shard_map(
        per_device,
        mesh=mesh,
        in_specs=(
            P(("rep", "ep"), None, None),
            P(("rep", "ep"), None),
            P(("rep", "ep"), None),
            P("rep", "ep", None, None, None, None),
            P("ep", None, None, None, None),
        ),
        out_specs=(P(("rep", "ep"), None, None), P("ep", None, None, None, None)),
        check_vma=False,
    )
```

```python
import functools

import jax
import jax.numpy as jnp
from jax import lax
from jax.experimental import pallas as pl
from jax.experimental.pallas import tpu as pltpu
from jax.sharding import PartitionSpec as P

SIDE = 16
CELLS = 256
GROUPS = 4
WIDTH = 32
CHANNELS = 128
NZ, NY, NC, NX = 8, 4, 2, 4
PIECE = 80
DEPTH = 8
BATCH = 4


def ep_perm(dz, dy, dc):
    pairs = []
    for z in range(NZ):
        for y in range(NY):
            for c in range(NC):
                to = ((z + dz) % NZ, (y + dy) % NY, c ^ dc)
                pairs.append(((z * NY + y) * NC + c, (to[0] * NY + to[1]) * NC + to[2]))
    return pairs


def rep_perm(dx):
    return [(x, (x + dx) % NX) for x in range(NX)]


def shifted(values, row_step, col_step, cell):
    if row_step == 0 and col_step == 0:
        return values
    rolled = pltpu.roll(values, (-(row_step * SIDE + col_step)) % CELLS, 1)
    row, col = cell // SIDE + row_step, cell % SIDE + col_step
    inside = (row >= 0) & (row < SIDE) & (col >= 0) & (col < SIDE)
    return jnp.where(inside, rolled, jnp.zeros_like(rolled))


def input_kernel(place_ref, gate_ref, grad_ref, weight_ref, out_ref, lhs_ref, rhs_ref, stage_ref):
    cell = lax.broadcasted_iota(jnp.int32, (1, CELLS), 1)
    lane_group = lax.broadcasted_iota(jnp.int32, (WIDTH, CHANNELS), 1) // WIDTH
    for j in range(BATCH):
        patch = pl.program_id(0) * BATCH + j
        grad = grad_ref[j]
        for b in (-1, 0, 1):
            by_col = shifted(grad, 0, -b, cell)
            for a in (-1, 0, 1):
                tap = 3 * (a + 1) + (b + 1)
                rhs_ref[j, tap * CHANNELS : (tap + 1) * CHANNELS, :] = shifted(by_col, -a, 0, cell)
        for k in range(2):
            for quarter in range(NX):
                stage_ref[j, k, quarter * PIECE : (quarter + 1) * PIECE, :] = weight_ref[
                    place_ref[(patch * 2 + k) * NX + quarter]
                ]
            for tap in range(9):
                kernel = stage_ref[j, k, tap * WIDTH : (tap + 1) * WIDTH, :]
                for group in range(GROUPS):
                    row = k * CHANNELS + group * WIDTH
                    lhs_ref[
                        j, row : row + WIDTH, tap * CHANNELS : (tap + 1) * CHANNELS
                    ] = jnp.where(lane_group == group, kernel, jnp.zeros_like(kernel))
        both = jnp.dot(lhs_ref[j], rhs_ref[j], preferred_element_type=jnp.float32)
        total = (
            gate_ref[patch * 2] * both[:CHANNELS] + gate_ref[patch * 2 + 1] * both[CHANNELS:]
        )
        out_ref[j] = total.astype(jnp.bfloat16)


def input_grads(place, gate, grad, weight):
    count = grad.shape[0]
    return pl.pallas_call(
        input_kernel,
        out_shape=jax.ShapeDtypeStruct(grad.shape, jnp.bfloat16),
        grid=(count // BATCH,),
        in_specs=[
            pl.BlockSpec(memory_space=pltpu.SMEM),
            pl.BlockSpec(memory_space=pltpu.SMEM),
            pl.BlockSpec((BATCH, CHANNELS, CELLS), lambda i: (i, 0, 0)),
            pl.BlockSpec(memory_space=pltpu.VMEM),
        ],
        out_specs=pl.BlockSpec((BATCH, CHANNELS, CELLS), lambda i: (i, 0, 0)),
        scratch_shapes=[
            pltpu.VMEM((BATCH, 2 * CHANNELS, 9 * CHANNELS), jnp.bfloat16),
            pltpu.VMEM((BATCH, 9 * CHANNELS, CELLS), jnp.bfloat16),
            pltpu.VMEM((BATCH, 2, NX * PIECE, CHANNELS), jnp.bfloat16),
        ],
        compiler_params=pltpu.CompilerParams(vmem_limit_bytes=28 << 20),
        cost_estimate=pl.CostEstimate(flops=1, bytes_accessed=1, transcendentals=0),
    )(place, gate, grad, weight)


def weight_kernel(chunks, plan, gate_of, grads, *refs):
    stash, out_refs, refs = refs[:chunks], refs[chunks : 2 * chunks], refs[2 * chunks :]
    grad_buf, stash_buf, lhs_a, rhs_a, lhs_b, rhs_b, total, sems = refs
    cell = lax.broadcasted_iota(jnp.int32, (1, CELLS), 1)
    pairs = plan[0]

    def start(pair):
        for j in range(2):
            slot = (pair % DEPTH) * 2 + j
            pltpu.make_async_copy(
                grads.at[plan[pair * 5 + 2 + j]], grad_buf.at[slot], sems.at[slot, 0]
            ).start()
        for chunk in range(chunks):

            @pl.when(plan[pair * 5 + 1] == chunk)
            def _(chunk=chunk):
                for j in range(2):
                    slot = (pair % DEPTH) * 2 + j
                    pltpu.make_async_copy(
                        stash[chunk].at[plan[pair * 5 + 4 + j]], stash_buf.at[slot], sems.at[slot, 1]
                    ).start()

    def finish(pair):
        for j in range(2):
            slot = (pair % DEPTH) * 2 + j
            pltpu.make_async_copy(grads.at[0], grad_buf.at[slot], sems.at[slot, 0]).wait()
            pltpu.make_async_copy(stash[0].at[0], stash_buf.at[slot], sems.at[slot, 1]).wait()

    def prepare(pair, lhs, rhs):
        for j in range(2):
            slot = (pair % DEPTH) * 2 + j
            cells = slice(j * CELLS, (j + 1) * CELLS)
            grad = grad_buf[slot].astype(jnp.float32) * gate_of[pair * 2 + j]
            grad = grad.astype(jnp.bfloat16)
            kept = stash_buf[slot]
            for i, step_by in enumerate((-1, 0, 1)):
                left = shifted(grad, -step_by, 0, cell)
                right = shifted(kept, 0, step_by, cell)
                for group in range(GROUPS):
                    rows = slice(group * WIDTH, (group + 1) * WIDTH)
                    lhs[group, i * WIDTH : (i + 1) * WIDTH, cells] = left[rows]
                    rhs[group, i * WIDTH : (i + 1) * WIDTH, cells] = right[rows]

    def multiply(pair, lhs, rhs):
        chunk = plan[pair * 5 + 1]
        for group in range(GROUPS):
            total[chunk, group] += lax.dot_general(
                lhs[group],
                rhs[group],
                (((1,), (1,)), ((), ())),
                preferred_element_type=jnp.float32,
            )

    for pair in range(DEPTH):

        @pl.when(pair < pairs)
        def _(pair=pair):
            start(jnp.int32(pair))

    total[...] = jnp.zeros_like(total)

    @pl.when(pairs > 0)
    def _():
        finish(jnp.int32(0))
        prepare(jnp.int32(0), lhs_a, rhs_a)

        @pl.when(DEPTH < pairs)
        def _():
            start(jnp.int32(DEPTH))

    def step(twice, carry):
        pair = twice * 2 + 1
        finish(pair)
        multiply(pair - 1, lhs_a, rhs_a)
        prepare(pair, lhs_b, rhs_b)

        @pl.when(pair + DEPTH < pairs)
        def _():
            start(pair + DEPTH)

        @pl.when(pair + 1 < pairs)
        def _():
            finish(pair + 1)

        multiply(pair, lhs_b, rhs_b)
        prepare(pair + 1, lhs_a, rhs_a)

        @pl.when(pair + 1 + DEPTH < pairs)
        def _():
            start(pair + 1 + DEPTH)

        return carry

    lax.fori_loop(0, pairs // 2, step, 0)
    for chunk in range(chunks):
        out_refs[chunk][...] = total[chunk].astype(out_refs[chunk].dtype)


def compact(row_of, gate_of):
    chunks, slots = row_of.shape
    length = chunks * slots
    used = row_of >= 0
    order = jnp.arange(slots, dtype=jnp.int32)
    rank = jnp.sum((used[:, :, None] & (order[:, None] < order[None, :])[None]).astype(jnp.int32), 1)
    padded = (jnp.sum(used.astype(jnp.int32), 1) + 1) // 2 * 2
    index = jnp.arange(chunks, dtype=jnp.int32)
    ends = jnp.sum(jnp.where(index[:, None] <= index[None, :], padded[:, None], 0), 0)
    where = (ends - padded)[:, None] + rank
    place = jnp.arange(length + 4, dtype=jnp.int32)
    hit = (used[:, :, None] & (where[:, :, None] == place)).astype(jnp.int32)
    rows = jnp.sum(hit * jnp.maximum(row_of, 0)[:, :, None], (0, 1))
    slot = jnp.sum(hit * order[None, :, None], (0, 1))
    gate = jnp.sum(jnp.where(hit > 0, gate_of[:, :, None], 0.0), (0, 1))
    chunk = jnp.sum((place[None, ::2] >= ends[:, None]).astype(jnp.int32), 0)
    chunk = jnp.minimum(chunk, chunks - 1)
    count = (ends[-1:] // 2 + 1) // 2 * 2
    pairs = jnp.concatenate([chunk[:, None], rows.reshape(-1, 2), slot.reshape(-1, 2)], 1)
    return jnp.concatenate([count, pairs.reshape(-1)]), gate


def weight_grads(plan, gate_of, grads, stash):
    chunks = len(stash)
    place = pl.BlockSpec(memory_space=pl.ANY)
    operand = pltpu.VMEM((GROUPS, 3 * WIDTH, 2 * CELLS), jnp.bfloat16)
    return pl.pallas_call(
        functools.partial(weight_kernel, chunks),
        out_shape=[jax.ShapeDtypeStruct((GROUPS, 3 * WIDTH, 3 * WIDTH), jnp.bfloat16)] * chunks,
        in_specs=[pl.BlockSpec(memory_space=pltpu.SMEM)] * 2 + [place] * (1 + chunks),
        out_specs=[pl.BlockSpec(memory_space=pltpu.VMEM)] * chunks,
        scratch_shapes=[
            pltpu.VMEM((2 * DEPTH, CHANNELS, CELLS), jnp.bfloat16),
            pltpu.VMEM((2 * DEPTH, CHANNELS, CELLS), jnp.bfloat16),
            operand,
            operand,
            operand,
            operand,
            pltpu.VMEM((chunks, GROUPS, 3 * WIDTH, 3 * WIDTH), jnp.float32),
            pltpu.SemaphoreType.DMA((2 * DEPTH, 2)),
        ],
        compiler_params=pltpu.CompilerParams(vmem_limit_bytes=56 << 20),
        cost_estimate=pl.CostEstimate(flops=1, bytes_accessed=1, transcendentals=0),
    )(plan, gate_of, grads, *stash)


def stack_of(first, others):
    return jnp.concatenate([first[None]] + [o[None] for o in others], 0)


def per_device(out_grad, routes, gates, stash, weights):
    x, e = lax.axis_index("rep"), lax.axis_index("ep")
    z, y, c = e // (NY * NC), e // NC % NY, e % NC
    rows, top = routes.shape
    groups = [[zz * NY * NC + r for zz in range(NZ)] for r in range(NY * NC)]
    grads = lax.all_gather(out_grad, "ep", axis=0, tiled=True, axis_index_groups=groups)

    kept = stash.reshape(NZ, NY, NC, 2, CHANNELS, CELLS)
    offsets = [(0, 0), (0, 1), (1, 0), (3, 0), (1, 1), (3, 1), (2, 0), (2, 1)]

    def sent(kept, d, dc):
        part = lax.dynamic_slice(
            kept, (0, (y + d) % NY, c ^ dc, 0, 0, 0), (NZ, 1, 1, 2, CHANNELS, CELLS)
        )
        return part.reshape(NZ * 2, CHANNELS, CELLS)

    first = [sent(kept, d, dc) for d, dc in offsets[2:4]]
    weights, *first = lax.optimization_barrier((weights, *first))
    mixed = weights[0].transpose(0, 3, 1, 2).reshape(9 * WIDTH, CHANNELS)
    mixed = jnp.pad(mixed, ((0, NX * PIECE - 9 * WIDTH), (0, 0)))
    piece = lax.dynamic_slice_in_dim(mixed, x * PIECE, PIECE, 0)
    note = jnp.concatenate(
        [routes.reshape(1, -1).astype(jnp.bfloat16), gates.reshape(1, -1)], 1
    )
    note = jnp.pad(note, ((0, 15), (0, CHANNELS - 2 * rows * top)))
    held = jnp.concatenate([piece, note], 0)
    kept, held, *first = lax.optimization_barrier((kept, held, *first))
    own, *rest = [sent(kept, d, dc) for d, dc in offsets[:2] + offsets[4:]]
    experts = [e - y * NC - c + ((y - d) % NY) * NC + (c ^ dc) for d, dc in offsets]
    experts = jnp.stack(experts)

    up = down = held
    from_z = {0: held}
    for d in range(1, NZ // 2 + 1):
        up = lax.ppermute(up, "ep", ep_perm(1, 0, 0))
        from_z[d] = up
        if d < NZ // 2:
            down = lax.ppermute(down, "ep", ep_perm(-1, 0, 0))
            from_z[NZ - d] = down
    held = jnp.stack([from_z[d] for d in range(NZ)])
    notes = held[:, PIECE, : 2 * rows * top].astype(jnp.float32)
    held = held[:, :PIECE]
    held, *rest = lax.optimization_barrier((held, *rest))
    rest = rest[:1] + first + rest[1:]
    chunks = [own] + [
        lax.ppermute(part, "ep", ep_perm(0, d, dc)) for part, (d, dc) in zip(rest, offsets[1:])
    ]
    held = stack_of(held, [lax.ppermute(held, "ep", ep_perm(0, d, 0)) for d in range(1, NY)])
    held = held.reshape(NY * NZ, PIECE, CHANNELS)
    held, chunks[2], chunks[3] = lax.optimization_barrier((held, chunks[2], chunks[3]))
    quarters = [held] + [lax.ppermute(held, "rep", rep_perm(d)) for d in range(1, NX)]
    quarters[2], chunks[4], chunks[5] = lax.optimization_barrier(
        (quarters[2], chunks[4], chunks[5])
    )
    quarters += [lax.ppermute(quarter, "ep", ep_perm(0, 0, 1)) for quarter in quarters]
    held = jnp.concatenate(quarters, 0)
    held, chunks[6] = lax.optimization_barrier((held, chunks[6]))
    held = held.reshape(NC * NX * NY * NZ, PIECE, CHANNELS)

    from_z = (z - jnp.arange(NZ, dtype=jnp.int32)) % NZ
    notes = jnp.sum(
        jnp.where((from_z[:, None] == jnp.arange(NZ)[None])[:, :, None], notes[:, None], 0.0), 0
    )
    named = notes[:, : rows * top].astype(jnp.int32)
    gate = notes[:, rows * top :]
    here = experts[:, None, None] == named[None]
    order = jnp.arange(rows * top, dtype=jnp.int32)
    before = (order[:, None] < order[None, :])[None, None] & here[:, :, :, None]
    earlier = jnp.sum(before.astype(jnp.int32), 2)
    chosen = here[:, :, None, :] & (earlier[:, :, None, :] == jnp.arange(2)[None, None, :, None])
    source_row = jnp.arange(NZ, dtype=jnp.int32)[:, None] * rows + (order // top)[None]
    row_of = jnp.max(jnp.where(chosen, source_row[None, :, None, :], -1), 3)
    gate_of = jnp.sum(jnp.where(chosen, gate[None, :, None, :], 0.0), 3)
    row_of, gate_of = row_of.reshape(8, NZ * 2), gate_of.reshape(8, NZ * 2)
    early, late = compact(row_of[:7], gate_of[:7]), compact(row_of[7:], gate_of[7:])
    flat = routes.reshape(-1)
    at_z, at_y, at_c = flat // (NY * NC), flat // NC % NY, flat % NC
    block = ((y - at_y) % NY) * NZ + (z - at_z) % NZ
    quarter = (x - jnp.arange(NX, dtype=jnp.int32)) % NX
    place = ((at_c ^ c)[:, None] * NX + quarter[None]) * (NZ * NY) + block[:, None]
    parts = list(weight_grads(*early, grads, chunks[:7]))
    parts[0], place = lax.optimization_barrier((parts[0], place))
    in_grad = input_grads(
        place.reshape(-1), gates.reshape(-1).astype(jnp.float32), out_grad, held
    )

    def returned(part, d, dc):
        if d or dc:
            part = lax.ppermute(part, "ep", ep_perm(0, -d, dc))
        return part.astype(jnp.float32)

    total = sum(returned(part, *offset) for part, offset in zip(parts, offsets))
    in_grad, total, plan = lax.optimization_barrier((in_grad, total, late[0]))
    (last,) = weight_grads(plan, late[1], grads, chunks[7:])
    total = total + returned(last, *offsets[7])
    total = total.astype(jnp.bfloat16)
    summed = total.astype(jnp.float32)
    for d in range(1, NX):
        summed = summed + lax.ppermute(total, "rep", rep_perm(d)).astype(jnp.float32)
    weight_grad = summed.reshape(GROUPS, 3, WIDTH, 3, WIDTH).transpose(1, 3, 0, 2, 4)
    return in_grad, weight_grad.reshape(1, 9, GROUPS, WIDTH, WIDTH)


def solution(mesh):
    return jax.shard_map(
        per_device,
        mesh=mesh,
        in_specs=(
            P(("rep", "ep"), None, None),
            P(("rep", "ep"), None),
            P(("rep", "ep"), None),
            P("rep", "ep", None, None, None, None),
            P("ep", None, None, None, None),
        ),
        out_specs=(P(("rep", "ep"), None, None), P("ep", None, None, None, None)),
        check_vma=False,
    )
```

```python
import functools

import jax
import jax.numpy as jnp
from jax import lax
from jax.experimental import pallas as pl
from jax.experimental.pallas import tpu as pltpu
from jax.sharding import PartitionSpec as P

SIDE = 16
CELLS = 256
GROUPS = 4
WIDTH = 32
CHANNELS = 128
NZ, NY, NC, NX = 8, 4, 2, 4
PIECE = 80
DEPTH = 8
BATCH = 4


def ep_perm(dz, dy, dc):
    pairs = []
    for z in range(NZ):
        for y in range(NY):
            for c in range(NC):
                to = ((z + dz) % NZ, (y + dy) % NY, c ^ dc)
                pairs.append(((z * NY + y) * NC + c, (to[0] * NY + to[1]) * NC + to[2]))
    return pairs


def rep_perm(dx):
    return [(x, (x + dx) % NX) for x in range(NX)]


def shifted(values, row_step, col_step, cell):
    if row_step == 0 and col_step == 0:
        return values
    rolled = pltpu.roll(values, (-(row_step * SIDE + col_step)) % CELLS, 1)
    row, col = cell // SIDE + row_step, cell % SIDE + col_step
    inside = (row >= 0) & (row < SIDE) & (col >= 0) & (col < SIDE)
    return jnp.where(inside, rolled, jnp.zeros_like(rolled))


def input_kernel(place_ref, gate_ref, grad_ref, weight_ref, out_ref, lhs_ref, rhs_ref, stage_ref):
    cell = lax.broadcasted_iota(jnp.int32, (1, CELLS), 1)
    lane_group = lax.broadcasted_iota(jnp.int32, (WIDTH, CHANNELS), 1) // WIDTH
    for j in range(BATCH):
        patch = pl.program_id(0) * BATCH + j
        grad = grad_ref[j]
        for b in (-1, 0, 1):
            by_col = shifted(grad, 0, -b, cell)
            for a in (-1, 0, 1):
                tap = 3 * (a + 1) + (b + 1)
                rhs_ref[j, tap * CHANNELS : (tap + 1) * CHANNELS, :] = shifted(by_col, -a, 0, cell)
        for k in range(2):
            for quarter in range(NX):
                stage_ref[j, k, quarter * PIECE : (quarter + 1) * PIECE, :] = weight_ref[
                    place_ref[(patch * 2 + k) * NX + quarter]
                ]
            for tap in range(9):
                kernel = stage_ref[j, k, tap * WIDTH : (tap + 1) * WIDTH, :]
                for group in range(GROUPS):
                    row = k * CHANNELS + group * WIDTH
                    lhs_ref[
                        j, row : row + WIDTH, tap * CHANNELS : (tap + 1) * CHANNELS
                    ] = jnp.where(lane_group == group, kernel, jnp.zeros_like(kernel))
        both = jnp.dot(lhs_ref[j], rhs_ref[j], preferred_element_type=jnp.float32)
        total = (
            gate_ref[patch * 2] * both[:CHANNELS] + gate_ref[patch * 2 + 1] * both[CHANNELS:]
        )
        out_ref[j] = total.astype(jnp.bfloat16)


def input_grads(place, gate, grad, weight):
    count = grad.shape[0]
    return pl.pallas_call(
        input_kernel,
        out_shape=jax.ShapeDtypeStruct(grad.shape, jnp.bfloat16),
        grid=(count // BATCH,),
        in_specs=[
            pl.BlockSpec(memory_space=pltpu.SMEM),
            pl.BlockSpec(memory_space=pltpu.SMEM),
            pl.BlockSpec((BATCH, CHANNELS, CELLS), lambda i: (i, 0, 0)),
            pl.BlockSpec(memory_space=pltpu.VMEM),
        ],
        out_specs=pl.BlockSpec((BATCH, CHANNELS, CELLS), lambda i: (i, 0, 0)),
        scratch_shapes=[
            pltpu.VMEM((BATCH, 2 * CHANNELS, 9 * CHANNELS), jnp.bfloat16),
            pltpu.VMEM((BATCH, 9 * CHANNELS, CELLS), jnp.bfloat16),
            pltpu.VMEM((BATCH, 2, NX * PIECE, CHANNELS), jnp.bfloat16),
        ],
        compiler_params=pltpu.CompilerParams(vmem_limit_bytes=28 << 20),
        cost_estimate=pl.CostEstimate(flops=1, bytes_accessed=1, transcendentals=0),
    )(place, gate, grad, weight)


def weight_kernel(lies, plan, gate_of, grads, *refs):
    chunks, arrays = len(lies), max(array for array, _ in lies) + 1
    stash, out_refs, refs = refs[:arrays], refs[arrays : arrays + chunks], refs[arrays + chunks :]
    grad_buf, stash_buf, lhs_a, rhs_a, lhs_b, rhs_b, total, sems = refs
    cell = lax.broadcasted_iota(jnp.int32, (1, CELLS), 1)
    pairs = plan[0]

    def start(pair):
        for j in range(2):
            slot = (pair % DEPTH) * 2 + j
            pltpu.make_async_copy(
                grads.at[plan[pair * 5 + 2 + j]], grad_buf.at[slot], sems.at[slot, 0]
            ).start()
        for chunk in range(chunks):

            @pl.when(plan[pair * 5 + 1] == chunk)
            def _(chunk=chunk):
                for j in range(2):
                    slot = (pair % DEPTH) * 2 + j
                    pltpu.make_async_copy(
                        stash[lies[chunk][0]].at[plan[pair * 5 + 4 + j] + lies[chunk][1]],
                        stash_buf.at[slot], sems.at[slot, 1]
                    ).start()

    def finish(pair):
        for j in range(2):
            slot = (pair % DEPTH) * 2 + j
            pltpu.make_async_copy(grads.at[0], grad_buf.at[slot], sems.at[slot, 0]).wait()
            pltpu.make_async_copy(stash[0].at[0], stash_buf.at[slot], sems.at[slot, 1]).wait()

    def prepare(pair, lhs, rhs):
        for j in range(2):
            slot = (pair % DEPTH) * 2 + j
            cells = slice(j * CELLS, (j + 1) * CELLS)
            grad = grad_buf[slot].astype(jnp.float32) * gate_of[pair * 2 + j]
            grad = grad.astype(jnp.bfloat16)
            kept = stash_buf[slot]
            for i, step_by in enumerate((-1, 0, 1)):
                left = shifted(grad, -step_by, 0, cell)
                right = shifted(kept, 0, step_by, cell)
                for group in range(GROUPS):
                    rows = slice(group * WIDTH, (group + 1) * WIDTH)
                    lhs[group, i * WIDTH : (i + 1) * WIDTH, cells] = left[rows]
                    rhs[group, i * WIDTH : (i + 1) * WIDTH, cells] = right[rows]

    def multiply(pair, lhs, rhs):
        chunk = plan[pair * 5 + 1]
        for group in range(GROUPS):
            total[chunk, group] += lax.dot_general(
                lhs[group],
                rhs[group],
                (((1,), (1,)), ((), ())),
                preferred_element_type=jnp.float32,
            )

    for pair in range(DEPTH):

        @pl.when(pair < pairs)
        def _(pair=pair):
            start(jnp.int32(pair))

    total[...] = jnp.zeros_like(total)

    @pl.when(pairs > 0)
    def _():
        finish(jnp.int32(0))
        prepare(jnp.int32(0), lhs_a, rhs_a)

        @pl.when(DEPTH < pairs)
        def _():
            start(jnp.int32(DEPTH))

    def step(twice, carry):
        pair = twice * 2 + 1
        finish(pair)
        multiply(pair - 1, lhs_a, rhs_a)
        prepare(pair, lhs_b, rhs_b)

        @pl.when(pair + DEPTH < pairs)
        def _():
            start(pair + DEPTH)

        @pl.when(pair + 1 < pairs)
        def _():
            finish(pair + 1)

        multiply(pair, lhs_b, rhs_b)
        prepare(pair + 1, lhs_a, rhs_a)

        @pl.when(pair + 1 + DEPTH < pairs)
        def _():
            start(pair + 1 + DEPTH)

        return carry

    lax.fori_loop(0, pairs // 2, step, 0)
    for chunk in range(chunks):
        out_refs[chunk][...] = total[chunk].astype(out_refs[chunk].dtype)


def compact(row_of, gate_of):
    chunks, slots = row_of.shape
    length = chunks * slots
    used = row_of >= 0
    order = jnp.arange(slots, dtype=jnp.int32)
    rank = jnp.sum((used[:, :, None] & (order[:, None] < order[None, :])[None]).astype(jnp.int32), 1)
    padded = (jnp.sum(used.astype(jnp.int32), 1) + 1) // 2 * 2
    index = jnp.arange(chunks, dtype=jnp.int32)
    ends = jnp.sum(jnp.where(index[:, None] <= index[None, :], padded[:, None], 0), 0)
    where = (ends - padded)[:, None] + rank
    place = jnp.arange(length + 4, dtype=jnp.int32)
    hit = (used[:, :, None] & (where[:, :, None] == place)).astype(jnp.int32)
    rows = jnp.sum(hit * jnp.maximum(row_of, 0)[:, :, None], (0, 1))
    slot = jnp.sum(hit * order[None, :, None], (0, 1))
    gate = jnp.sum(jnp.where(hit > 0, gate_of[:, :, None], 0.0), (0, 1))
    chunk = jnp.sum((place[None, ::2] >= ends[:, None]).astype(jnp.int32), 0)
    chunk = jnp.minimum(chunk, chunks - 1)
    count = (ends[-1:] // 2 + 1) // 2 * 2
    pairs = jnp.concatenate([chunk[:, None], rows.reshape(-1, 2), slot.reshape(-1, 2)], 1)
    return jnp.concatenate([count, pairs.reshape(-1)]), gate


def weight_grads(plan, gate_of, grads, stash, lies):
    chunks = len(lies)
    place = pl.BlockSpec(memory_space=pl.ANY)
    operand = pltpu.VMEM((GROUPS, 3 * WIDTH, 2 * CELLS), jnp.bfloat16)
    return pl.pallas_call(
        functools.partial(weight_kernel, lies),
        out_shape=[jax.ShapeDtypeStruct((GROUPS, 3 * WIDTH, 3 * WIDTH), jnp.bfloat16)] * chunks,
        in_specs=[pl.BlockSpec(memory_space=pltpu.SMEM)] * 2 + [place] * (1 + len(stash)),
        out_specs=[pl.BlockSpec(memory_space=pltpu.VMEM)] * chunks,
        scratch_shapes=[
            pltpu.VMEM((2 * DEPTH, CHANNELS, CELLS), jnp.bfloat16),
            pltpu.VMEM((2 * DEPTH, CHANNELS, CELLS), jnp.bfloat16),
            operand,
            operand,
            operand,
            operand,
            pltpu.VMEM((chunks, GROUPS, 3 * WIDTH, 3 * WIDTH), jnp.float32),
            pltpu.SemaphoreType.DMA((2 * DEPTH, 2)),
        ],
        compiler_params=pltpu.CompilerParams(vmem_limit_bytes=56 << 20),
        cost_estimate=pl.CostEstimate(flops=1, bytes_accessed=1, transcendentals=0),
    )(plan, gate_of, grads, *stash)


def stack_of(first, others):
    return jnp.concatenate([first[None]] + [o[None] for o in others], 0)


def per_device(out_grad, routes, gates, stash, weights):
    x, e = lax.axis_index("rep"), lax.axis_index("ep")
    z, y, c = e // (NY * NC), e // NC % NY, e % NC
    rows, top = routes.shape
    groups = [[zz * NY * NC + r for zz in range(NZ)] for r in range(NY * NC)]
    grads = lax.all_gather(out_grad, "ep", axis=0, tiled=True, axis_index_groups=groups)

    kept = stash.reshape(NZ, NY, NC, 2, CHANNELS, CELLS)
    offsets = [(0, 0), (0, 1), (1, 0), (3, 0), (1, 1), (3, 1), (2, 0), (2, 1)]

    def sent(kept, d, dc):
        part = lax.dynamic_slice(
            kept, (0, (y + d) % NY, c ^ dc, 0, 0, 0), (NZ, 1, 1, 2, CHANNELS, CELLS)
        )
        return part.reshape(NZ * 2, CHANNELS, CELLS)

    def along(part, d, dc):
        return lax.ppermute(part, "ep", ep_perm(0, d, dc))

    mixed = weights[0].transpose(0, 3, 1, 2).reshape(9 * WIDTH, CHANNELS)
    mixed = jnp.pad(mixed, ((0, NX * PIECE - 9 * WIDTH), (0, 0)))
    held = lax.dynamic_slice_in_dim(mixed, x * PIECE, PIECE, 0)
    next_to = [sent(kept, d, dc) for d, dc in offsets[2:4]]
    kept, held, *next_to = lax.optimization_barrier((kept, held, *next_to))
    next_to += [sent(kept, d, dc) for d, dc in offsets[4:6]]
    next_to = [along(part, d, dc) for part, (d, dc) in zip(next_to, offsets[2:6])]
    experts = [e - y * NC - c + ((y - d) % NY) * NC + (c ^ dc) for d, dc in offsets]
    experts = jnp.stack(experts)

    held = stack_of(held, [along(held, d, 0) for d in range(1, NY)])
    note = jnp.concatenate(
        [routes.reshape(1, -1).astype(jnp.bfloat16), gates.reshape(1, -1)], 1
    )
    note = jnp.pad(note, ((0, 15), (0, CHANNELS - 2 * rows * top)))
    held = jnp.concatenate([held.reshape(NY * PIECE, CHANNELS), note], 0)

    kept, held = lax.optimization_barrier((kept, held))
    swapped = along(jnp.concatenate([sent(kept, 0, 1), sent(kept, 2, 1)], 0), 0, 1)
    across = along(jnp.concatenate([sent(kept, 2, 0), swapped[NZ * 2 :]], 0), 2, 0)

    up = down = held
    from_z = {0: held}
    for d in range(1, NZ // 2 + 1):
        up = lax.ppermute(up, "ep", ep_perm(1, 0, 0))
        from_z[d] = up
        if d < NZ // 2:
            down = lax.ppermute(down, "ep", ep_perm(-1, 0, 0))
            from_z[NZ - d] = down
    held = jnp.stack([from_z[d] for d in range(NZ)])
    notes = held[:, NY * PIECE, : 2 * rows * top].astype(jnp.float32)
    held = held[:, : NY * PIECE].reshape(NZ * NY, PIECE, CHANNELS)
    held, *next_to = lax.optimization_barrier((held, *next_to))
    quarters = [held] + [lax.ppermute(held, "rep", rep_perm(d)) for d in range(1, NX)]
    quarters += [along(quarter, 0, 1) for quarter in quarters]
    held = jnp.concatenate(quarters, 0).reshape(NC * NX * NY * NZ, PIECE, CHANNELS)

    from_z = (z - jnp.arange(NZ, dtype=jnp.int32)) % NZ
    notes = jnp.sum(
        jnp.where((from_z[:, None] == jnp.arange(NZ)[None])[:, :, None], notes[:, None], 0.0), 0
    )
    named = notes[:, : rows * top].astype(jnp.int32)
    gate = notes[:, rows * top :]
    here = experts[:, None, None] == named[None]
    order = jnp.arange(rows * top, dtype=jnp.int32)
    before = (order[:, None] < order[None, :])[None, None] & here[:, :, :, None]
    earlier = jnp.sum(before.astype(jnp.int32), 2)
    chosen = here[:, :, None, :] & (earlier[:, :, None, :] == jnp.arange(2)[None, None, :, None])
    source_row = jnp.arange(NZ, dtype=jnp.int32)[:, None] * rows + (order // top)[None]
    row_of = jnp.max(jnp.where(chosen, source_row[None, :, None, :], -1), 3)
    gate_of = jnp.sum(jnp.where(chosen, gate[None, :, None, :], 0.0), 3)
    row_of, gate_of = row_of.reshape(8, NZ * 2), gate_of.reshape(8, NZ * 2)
    early, late = compact(row_of[:6], gate_of[:6]), compact(row_of[6:], gate_of[6:])
    flat = routes.reshape(-1)
    at_z, at_y, at_c = flat // (NY * NC), flat // NC % NY, flat % NC
    block = ((z - at_z) % NZ) * NY + (y - at_y) % NY
    quarter = (x - jnp.arange(NX, dtype=jnp.int32)) % NX
    place = ((at_c ^ c)[:, None] * NX + quarter[None]) * (NZ * NY) + block[:, None]
    in_grad = input_grads(
        place.reshape(-1), gates.reshape(-1).astype(jnp.float32), out_grad, held
    )
    in_grad, plan = lax.optimization_barrier((in_grad, early[0]))
    first = [sent(kept, 0, 0), swapped, *next_to]
    parts = weight_grads(plan, early[1], grads, first, tuple((i, 0) for i in range(6)))
    parts += weight_grads(*late, grads, [across], ((0, 0), (0, NZ * 2)))

    total = None
    for part, (d, dc) in zip(parts, offsets):
        part = (along(part, -d, dc) if d or dc else part).astype(jnp.float32)
        total = part if total is None else total + part
    total = total.astype(jnp.bfloat16)
    summed = total.astype(jnp.float32)
    for d in range(1, NX):
        summed = summed + lax.ppermute(total, "rep", rep_perm(d)).astype(jnp.float32)
    weight_grad = summed.reshape(GROUPS, 3, WIDTH, 3, WIDTH).transpose(1, 3, 0, 2, 4)
    return in_grad, weight_grad.reshape(1, 9, GROUPS, WIDTH, WIDTH)


def solution(mesh):
    return jax.shard_map(
        per_device,
        mesh=mesh,
        in_specs=(
            P(("rep", "ep"), None, None),
            P(("rep", "ep"), None),
            P(("rep", "ep"), None),
            P("rep", "ep", None, None, None, None),
            P("ep", None, None, None, None),
        ),
        out_specs=(P(("rep", "ep"), None, None), P("ep", None, None, None, None)),
        check_vma=False,
    )
```

```python
import functools

import jax
import jax.numpy as jnp
from jax import lax
from jax.experimental import pallas as pl
from jax.experimental.pallas import tpu as pltpu
from jax.sharding import PartitionSpec as P

SIDE = 16
CELLS = 256
GROUPS = 4
WIDTH = 32
CHANNELS = 128
NZ, NY, NC, NX = 8, 4, 2, 4
PIECE = 80
DEPTH = 8
BATCH = 4


def ep_perm(dz, dy, dc):
    pairs = []
    for z in range(NZ):
        for y in range(NY):
            for c in range(NC):
                to = ((z + dz) % NZ, (y + dy) % NY, c ^ dc)
                pairs.append(((z * NY + y) * NC + c, (to[0] * NY + to[1]) * NC + to[2]))
    return pairs


def rep_perm(dx):
    return [(x, (x + dx) % NX) for x in range(NX)]


def shifted(values, row_step, col_step, cell):
    if row_step == 0 and col_step == 0:
        return values
    rolled = pltpu.roll(values, (-(row_step * SIDE + col_step)) % CELLS, 1)
    row, col = cell // SIDE + row_step, cell % SIDE + col_step
    inside = (row >= 0) & (row < SIDE) & (col >= 0) & (col < SIDE)
    return jnp.where(inside, rolled, jnp.zeros_like(rolled))


def input_kernel(place_ref, gate_ref, grad_ref, weight_ref, out_ref, lhs_ref, rhs_ref, stage_ref):
    cell = lax.broadcasted_iota(jnp.int32, (1, CELLS), 1)
    lane_group = lax.broadcasted_iota(jnp.int32, (WIDTH, CHANNELS), 1) // WIDTH
    for j in range(BATCH):
        patch = pl.program_id(0) * BATCH + j
        grad = grad_ref[j]
        for b in (-1, 0, 1):
            by_col = shifted(grad, 0, -b, cell)
            for a in (-1, 0, 1):
                tap = 3 * (a + 1) + (b + 1)
                rhs_ref[j, tap * CHANNELS : (tap + 1) * CHANNELS, :] = shifted(by_col, -a, 0, cell)
        for k in range(2):
            for quarter in range(NX):
                stage_ref[j, k, quarter * PIECE : (quarter + 1) * PIECE, :] = weight_ref[
                    place_ref[(patch * 2 + k) * NX + quarter]
                ]
            for tap in range(9):
                kernel = stage_ref[j, k, tap * WIDTH : (tap + 1) * WIDTH, :]
                for group in range(GROUPS):
                    row = k * CHANNELS + group * WIDTH
                    lhs_ref[
                        j, row : row + WIDTH, tap * CHANNELS : (tap + 1) * CHANNELS
                    ] = jnp.where(lane_group == group, kernel, jnp.zeros_like(kernel))
        both = jnp.dot(lhs_ref[j], rhs_ref[j], preferred_element_type=jnp.float32)
        total = (
            gate_ref[patch * 2] * both[:CHANNELS] + gate_ref[patch * 2 + 1] * both[CHANNELS:]
        )
        out_ref[j] = total.astype(jnp.bfloat16)


def input_grads(place, gate, grad, weight):
    count = grad.shape[0]
    return pl.pallas_call(
        input_kernel,
        out_shape=jax.ShapeDtypeStruct(grad.shape, jnp.bfloat16),
        grid=(count // BATCH,),
        in_specs=[
            pl.BlockSpec(memory_space=pltpu.SMEM),
            pl.BlockSpec(memory_space=pltpu.SMEM),
            pl.BlockSpec((BATCH, CHANNELS, CELLS), lambda i: (i, 0, 0)),
            pl.BlockSpec(memory_space=pltpu.VMEM),
        ],
        out_specs=pl.BlockSpec((BATCH, CHANNELS, CELLS), lambda i: (i, 0, 0)),
        scratch_shapes=[
            pltpu.VMEM((BATCH, 2 * CHANNELS, 9 * CHANNELS), jnp.bfloat16),
            pltpu.VMEM((BATCH, 9 * CHANNELS, CELLS), jnp.bfloat16),
            pltpu.VMEM((BATCH, 2, NX * PIECE, CHANNELS), jnp.bfloat16),
        ],
        compiler_params=pltpu.CompilerParams(vmem_limit_bytes=28 << 20),
        cost_estimate=pl.CostEstimate(flops=1, bytes_accessed=1, transcendentals=0),
    )(place, gate, grad, weight)


def weight_kernel(chunks, plan, gate_of, grads, *refs):
    stash, out_refs, refs = refs[:chunks], refs[chunks : 2 * chunks], refs[2 * chunks :]
    grad_buf, stash_buf, lhs_a, rhs_a, lhs_b, rhs_b, total, sems = refs
    cell = lax.broadcasted_iota(jnp.int32, (1, CELLS), 1)
    pairs = plan[0]

    def start(pair):
        for j in range(2):
            slot = (pair % DEPTH) * 2 + j
            pltpu.make_async_copy(
                grads.at[plan[pair * 5 + 2 + j]], grad_buf.at[slot], sems.at[slot, 0]
            ).start()
        for chunk in range(chunks):

            @pl.when(plan[pair * 5 + 1] == chunk)
            def _(chunk=chunk):
                for j in range(2):
                    slot = (pair % DEPTH) * 2 + j
                    pltpu.make_async_copy(
                        stash[chunk].at[plan[pair * 5 + 4 + j]], stash_buf.at[slot], sems.at[slot, 1]
                    ).start()

    def finish(pair):
        for j in range(2):
            slot = (pair % DEPTH) * 2 + j
            pltpu.make_async_copy(grads.at[0], grad_buf.at[slot], sems.at[slot, 0]).wait()
            pltpu.make_async_copy(stash[0].at[0], stash_buf.at[slot], sems.at[slot, 1]).wait()

    def prepare(pair, lhs, rhs):
        for j in range(2):
            slot = (pair % DEPTH) * 2 + j
            cells = slice(j * CELLS, (j + 1) * CELLS)
            grad = grad_buf[slot].astype(jnp.float32) * gate_of[pair * 2 + j]
            grad = grad.astype(jnp.bfloat16)
            kept = stash_buf[slot]
            for i, step_by in enumerate((-1, 0, 1)):
                left = shifted(grad, -step_by, 0, cell)
                right = shifted(kept, 0, step_by, cell)
                for group in range(GROUPS):
                    rows = slice(group * WIDTH, (group + 1) * WIDTH)
                    lhs[group, i * WIDTH : (i + 1) * WIDTH, cells] = left[rows]
                    rhs[group, i * WIDTH : (i + 1) * WIDTH, cells] = right[rows]

    def multiply(pair, lhs, rhs):
        chunk = plan[pair * 5 + 1]
        for group in range(GROUPS):
            total[chunk, group] += lax.dot_general(
                lhs[group],
                rhs[group],
                (((1,), (1,)), ((), ())),
                preferred_element_type=jnp.float32,
            )

    for pair in range(DEPTH):

        @pl.when(pair < pairs)
        def _(pair=pair):
            start(jnp.int32(pair))

    total[...] = jnp.zeros_like(total)

    @pl.when(pairs > 0)
    def _():
        finish(jnp.int32(0))
        prepare(jnp.int32(0), lhs_a, rhs_a)

        @pl.when(DEPTH < pairs)
        def _():
            start(jnp.int32(DEPTH))

    def step(twice, carry):
        pair = twice * 2 + 1
        finish(pair)
        multiply(pair - 1, lhs_a, rhs_a)
        prepare(pair, lhs_b, rhs_b)

        @pl.when(pair + DEPTH < pairs)
        def _():
            start(pair + DEPTH)

        @pl.when(pair + 1 < pairs)
        def _():
            finish(pair + 1)

        multiply(pair, lhs_b, rhs_b)
        prepare(pair + 1, lhs_a, rhs_a)

        @pl.when(pair + 1 + DEPTH < pairs)
        def _():
            start(pair + 1 + DEPTH)

        return carry

    lax.fori_loop(0, pairs // 2, step, 0)
    for chunk in range(chunks):
        out_refs[chunk][...] = total[chunk].astype(out_refs[chunk].dtype)


def compact(row_of, gate_of):
    chunks, slots = row_of.shape
    length = chunks * slots
    used = row_of >= 0
    order = jnp.arange(slots, dtype=jnp.int32)
    rank = jnp.sum((used[:, :, None] & (order[:, None] < order[None, :])[None]).astype(jnp.int32), 1)
    padded = (jnp.sum(used.astype(jnp.int32), 1) + 1) // 2 * 2
    index = jnp.arange(chunks, dtype=jnp.int32)
    ends = jnp.sum(jnp.where(index[:, None] <= index[None, :], padded[:, None], 0), 0)
    where = (ends - padded)[:, None] + rank
    place = jnp.arange(length + 4, dtype=jnp.int32)
    hit = (used[:, :, None] & (where[:, :, None] == place)).astype(jnp.int32)
    rows = jnp.sum(hit * jnp.maximum(row_of, 0)[:, :, None], (0, 1))
    slot = jnp.sum(hit * order[None, :, None], (0, 1))
    gate = jnp.sum(jnp.where(hit > 0, gate_of[:, :, None], 0.0), (0, 1))
    chunk = jnp.sum((place[None, ::2] >= ends[:, None]).astype(jnp.int32), 0)
    chunk = jnp.minimum(chunk, chunks - 1)
    count = (ends[-1:] // 2 + 1) // 2 * 2
    pairs = jnp.concatenate([chunk[:, None], rows.reshape(-1, 2), slot.reshape(-1, 2)], 1)
    return jnp.concatenate([count, pairs.reshape(-1)]), gate


def weight_grads(plan, gate_of, grads, stash):
    chunks = len(stash)
    place = pl.BlockSpec(memory_space=pl.ANY)
    operand = pltpu.VMEM((GROUPS, 3 * WIDTH, 2 * CELLS), jnp.bfloat16)
    return pl.pallas_call(
        functools.partial(weight_kernel, chunks),
        out_shape=[jax.ShapeDtypeStruct((GROUPS, 3 * WIDTH, 3 * WIDTH), jnp.bfloat16)] * chunks,
        in_specs=[pl.BlockSpec(memory_space=pltpu.SMEM)] * 2 + [place] * (1 + chunks),
        out_specs=[pl.BlockSpec(memory_space=pltpu.VMEM)] * chunks,
        scratch_shapes=[
            pltpu.VMEM((2 * DEPTH, CHANNELS, CELLS), jnp.bfloat16),
            pltpu.VMEM((2 * DEPTH, CHANNELS, CELLS), jnp.bfloat16),
            operand,
            operand,
            operand,
            operand,
            pltpu.VMEM((chunks, GROUPS, 3 * WIDTH, 3 * WIDTH), jnp.float32),
            pltpu.SemaphoreType.DMA((2 * DEPTH, 2)),
        ],
        compiler_params=pltpu.CompilerParams(vmem_limit_bytes=56 << 20),
        cost_estimate=pl.CostEstimate(flops=1, bytes_accessed=1, transcendentals=0),
    )(plan, gate_of, grads, *stash)


def stack_of(first, others):
    return jnp.concatenate([first[None]] + [o[None] for o in others], 0)


def per_device(out_grad, routes, gates, stash, weights):
    x, e = lax.axis_index("rep"), lax.axis_index("ep")
    z, y, c = e // (NY * NC), e // NC % NY, e % NC
    rows, top = routes.shape
    groups = [[zz * NY * NC + r for zz in range(NZ)] for r in range(NY * NC)]
    grads = lax.all_gather(out_grad, "ep", axis=0, tiled=True, axis_index_groups=groups)

    kept = stash.reshape(NZ, NY, NC, 2, CHANNELS, CELLS)
    offsets = [(0, 0), (0, 1), (1, 0), (3, 0), (1, 1), (3, 1), (2, 0), (2, 1)]

    def sent(kept, d, dc):
        part = lax.dynamic_slice(
            kept, (0, (y + d) % NY, c ^ dc, 0, 0, 0), (NZ, 1, 1, 2, CHANNELS, CELLS)
        )
        return part.reshape(NZ * 2, CHANNELS, CELLS)

    first = [sent(kept, d, dc) for d, dc in offsets[2:4]]
    weights, *first = lax.optimization_barrier((weights, *first))
    mixed = weights[0].transpose(0, 3, 1, 2).reshape(9 * WIDTH, CHANNELS)
    mixed = jnp.pad(mixed, ((0, NX * PIECE - 9 * WIDTH), (0, 0)))
    piece = lax.dynamic_slice_in_dim(mixed, x * PIECE, PIECE, 0)
    note = jnp.concatenate(
        [routes.reshape(1, -1).astype(jnp.bfloat16), gates.reshape(1, -1)], 1
    )
    note = jnp.pad(note, ((0, 15), (0, CHANNELS - 2 * rows * top)))
    held = jnp.concatenate([piece, note], 0)
    kept, held, *first = lax.optimization_barrier((kept, held, *first))
    own, *rest = [sent(kept, d, dc) for d, dc in offsets[:2] + offsets[4:]]
    experts = [e - y * NC - c + ((y - d) % NY) * NC + (c ^ dc) for d, dc in offsets]
    experts = jnp.stack(experts)

    up = down = held
    from_z = {0: held}
    for d in range(1, NZ // 2 + 1):
        up = lax.ppermute(up, "ep", ep_perm(1, 0, 0))
        from_z[d] = up
        if d < NZ // 2:
            down = lax.ppermute(down, "ep", ep_perm(-1, 0, 0))
            from_z[NZ - d] = down
    held = jnp.stack([from_z[d] for d in range(NZ)])
    notes = held[:, PIECE, : 2 * rows * top].astype(jnp.float32)
    held = held[:, :PIECE]
    held, *rest = lax.optimization_barrier((held, *rest))
    rest = rest[:1] + first + rest[1:]
    chunks = [own] + [
        lax.ppermute(part, "ep", ep_perm(0, d, dc)) for part, (d, dc) in zip(rest, offsets[1:])
    ]
    held = stack_of(held, [lax.ppermute(held, "ep", ep_perm(0, d, 0)) for d in range(1, NY)])
    held = held.reshape(NY * NZ, PIECE, CHANNELS)
    held, chunks[2], chunks[3] = lax.optimization_barrier((held, chunks[2], chunks[3]))
    quarters = [held] + [lax.ppermute(held, "rep", rep_perm(d)) for d in range(1, NX)]
    quarters[2], chunks[4], chunks[5] = lax.optimization_barrier(
        (quarters[2], chunks[4], chunks[5])
    )
    quarters += [lax.ppermute(quarter, "ep", ep_perm(0, 0, 1)) for quarter in quarters]
    held = jnp.concatenate(quarters, 0)
    held = held.reshape(NC * NX * NY * NZ, PIECE, CHANNELS)

    from_z = (z - jnp.arange(NZ, dtype=jnp.int32)) % NZ
    notes = jnp.sum(
        jnp.where((from_z[:, None] == jnp.arange(NZ)[None])[:, :, None], notes[:, None], 0.0), 0
    )
    named = notes[:, : rows * top].astype(jnp.int32)
    gate = notes[:, rows * top :]
    here = experts[:, None, None] == named[None]
    order = jnp.arange(rows * top, dtype=jnp.int32)
    before = (order[:, None] < order[None, :])[None, None] & here[:, :, :, None]
    earlier = jnp.sum(before.astype(jnp.int32), 2)
    chosen = here[:, :, None, :] & (earlier[:, :, None, :] == jnp.arange(2)[None, None, :, None])
    source_row = jnp.arange(NZ, dtype=jnp.int32)[:, None] * rows + (order // top)[None]
    row_of = jnp.max(jnp.where(chosen, source_row[None, :, None, :], -1), 3)
    gate_of = jnp.sum(jnp.where(chosen, gate[None, :, None, :], 0.0), 3)
    row_of, gate_of = row_of.reshape(8, NZ * 2), gate_of.reshape(8, NZ * 2)
    early, late = compact(row_of[:7], gate_of[:7]), compact(row_of[7:], gate_of[7:])
    flat = routes.reshape(-1)
    at_z, at_y, at_c = flat // (NY * NC), flat // NC % NY, flat % NC
    block = ((y - at_y) % NY) * NZ + (z - at_z) % NZ
    quarter = (x - jnp.arange(NX, dtype=jnp.int32)) % NX
    place = ((at_c ^ c)[:, None] * NX + quarter[None]) * (NZ * NY) + block[:, None]
    in_grad = input_grads(
        place.reshape(-1), gates.reshape(-1).astype(jnp.float32), out_grad, held
    )
    in_grad, plan = lax.optimization_barrier((in_grad, early[0]))
    parts = weight_grads(plan, early[1], grads, chunks[:7])
    parts += weight_grads(*late, grads, chunks[7:])

    total = None
    for part, (d, dc) in zip(parts, offsets):
        if d or dc:
            part = lax.ppermute(part, "ep", ep_perm(0, -d, dc))
        part = part.astype(jnp.float32)
        total = part if total is None else total + part
    total = total.astype(jnp.bfloat16)
    summed = total.astype(jnp.float32)
    for d in range(1, NX):
        summed = summed + lax.ppermute(total, "rep", rep_perm(d)).astype(jnp.float32)
    weight_grad = summed.reshape(GROUPS, 3, WIDTH, 3, WIDTH).transpose(1, 3, 0, 2, 4)
    return in_grad, weight_grad.reshape(1, 9, GROUPS, WIDTH, WIDTH)


def solution(mesh):
    return jax.shard_map(
        per_device,
        mesh=mesh,
        in_specs=(
            P(("rep", "ep"), None, None),
            P(("rep", "ep"), None),
            P(("rep", "ep"), None),
            P("rep", "ep", None, None, None, None),
            P("ep", None, None, None, None),
        ),
        out_specs=(P(("rep", "ep"), None, None), P("ep", None, None, None, None)),
        check_vma=False,
    )
```

```python
import functools

import jax
import jax.numpy as jnp
from jax import lax
from jax.experimental import pallas as pl
from jax.experimental.pallas import tpu as pltpu
from jax.sharding import PartitionSpec as P

SIDE = 16
CELLS = 256
GROUPS = 4
WIDTH = 32
CHANNELS = 128
NZ, NY, NC, NX = 8, 4, 2, 4
PIECE = 80
DEPTH = 8
BATCH = 4


def ep_perm(dz, dy, dc):
    pairs = []
    for z in range(NZ):
        for y in range(NY):
            for c in range(NC):
                to = ((z + dz) % NZ, (y + dy) % NY, c ^ dc)
                pairs.append(((z * NY + y) * NC + c, (to[0] * NY + to[1]) * NC + to[2]))
    return pairs


def rep_perm(dx):
    return [(x, (x + dx) % NX) for x in range(NX)]


def shifted(values, row_step, col_step, cell):
    if row_step == 0 and col_step == 0:
        return values
    rolled = pltpu.roll(values, (-(row_step * SIDE + col_step)) % CELLS, 1)
    row, col = cell // SIDE + row_step, cell % SIDE + col_step
    inside = (row >= 0) & (row < SIDE) & (col >= 0) & (col < SIDE)
    return jnp.where(inside, rolled, jnp.zeros_like(rolled))


def input_kernel(place_ref, gate_ref, grad_ref, weight_ref, out_ref, lhs_ref, rhs_ref, stage_ref):
    cell = lax.broadcasted_iota(jnp.int32, (1, CELLS), 1)
    lane_group = lax.broadcasted_iota(jnp.int32, (WIDTH, CHANNELS), 1) // WIDTH
    for j in range(BATCH):
        patch = pl.program_id(0) * BATCH + j
        grad = grad_ref[j]
        for b in (-1, 0, 1):
            by_col = shifted(grad, 0, -b, cell)
            for a in (-1, 0, 1):
                tap = 3 * (a + 1) + (b + 1)
                rhs_ref[j, tap * CHANNELS : (tap + 1) * CHANNELS, :] = shifted(by_col, -a, 0, cell)
        for k in range(2):
            for quarter in range(NX):
                stage_ref[j, k, quarter * PIECE : (quarter + 1) * PIECE, :] = weight_ref[
                    place_ref[(patch * 2 + k) * NX + quarter]
                ]
            for tap in range(9):
                kernel = stage_ref[j, k, tap * WIDTH : (tap + 1) * WIDTH, :]
                for group in range(GROUPS):
                    row = k * CHANNELS + group * WIDTH
                    lhs_ref[
                        j, row : row + WIDTH, tap * CHANNELS : (tap + 1) * CHANNELS
                    ] = jnp.where(lane_group == group, kernel, jnp.zeros_like(kernel))
        both = jnp.dot(lhs_ref[j], rhs_ref[j], preferred_element_type=jnp.float32)
        total = (
            gate_ref[patch * 2] * both[:CHANNELS] + gate_ref[patch * 2 + 1] * both[CHANNELS:]
        )
        out_ref[j] = total.astype(jnp.bfloat16)


def input_grads(place, gate, grad, weight):
    count = grad.shape[0]
    return pl.pallas_call(
        input_kernel,
        out_shape=jax.ShapeDtypeStruct(grad.shape, jnp.bfloat16),
        grid=(count // BATCH,),
        in_specs=[
            pl.BlockSpec(memory_space=pltpu.SMEM),
            pl.BlockSpec(memory_space=pltpu.SMEM),
            pl.BlockSpec((BATCH, CHANNELS, CELLS), lambda i: (i, 0, 0)),
            pl.BlockSpec(memory_space=pltpu.VMEM),
        ],
        out_specs=pl.BlockSpec((BATCH, CHANNELS, CELLS), lambda i: (i, 0, 0)),
        scratch_shapes=[
            pltpu.VMEM((BATCH, 2 * CHANNELS, 9 * CHANNELS), jnp.bfloat16),
            pltpu.VMEM((BATCH, 9 * CHANNELS, CELLS), jnp.bfloat16),
            pltpu.VMEM((BATCH, 2, NX * PIECE, CHANNELS), jnp.bfloat16),
        ],
        compiler_params=pltpu.CompilerParams(vmem_limit_bytes=28 << 20),
        cost_estimate=pl.CostEstimate(flops=1, bytes_accessed=1, transcendentals=0),
    )(place, gate, grad, weight)


def weight_kernel(chunks, plan, gate_of, grads, *refs):
    stash, out_refs, refs = refs[:chunks], refs[chunks : 2 * chunks], refs[2 * chunks :]
    grad_buf, stash_buf, lhs_a, rhs_a, lhs_b, rhs_b, total, sems = refs
    cell = lax.broadcasted_iota(jnp.int32, (1, CELLS), 1)
    pairs = plan[0]

    def start(pair):
        for j in range(2):
            slot = (pair % DEPTH) * 2 + j
            pltpu.make_async_copy(
                grads.at[plan[pair * 5 + 2 + j]], grad_buf.at[slot], sems.at[slot, 0]
            ).start()
        for chunk in range(chunks):

            @pl.when(plan[pair * 5 + 1] == chunk)
            def _(chunk=chunk):
                for j in range(2):
                    slot = (pair % DEPTH) * 2 + j
                    pltpu.make_async_copy(
                        stash[chunk].at[plan[pair * 5 + 4 + j]], stash_buf.at[slot], sems.at[slot, 1]
                    ).start()

    def finish(pair):
        for j in range(2):
            slot = (pair % DEPTH) * 2 + j
            pltpu.make_async_copy(grads.at[0], grad_buf.at[slot], sems.at[slot, 0]).wait()
            pltpu.make_async_copy(stash[0].at[0], stash_buf.at[slot], sems.at[slot, 1]).wait()

    def prepare(pair, lhs, rhs):
        for j in range(2):
            slot = (pair % DEPTH) * 2 + j
            cells = slice(j * CELLS, (j + 1) * CELLS)
            grad = grad_buf[slot].astype(jnp.float32) * gate_of[pair * 2 + j]
            grad = grad.astype(jnp.bfloat16)
            kept = stash_buf[slot]
            for i, step_by in enumerate((-1, 0, 1)):
                left = shifted(grad, -step_by, 0, cell)
                right = shifted(kept, 0, step_by, cell)
                for group in range(GROUPS):
                    rows = slice(group * WIDTH, (group + 1) * WIDTH)
                    lhs[group, i * WIDTH : (i + 1) * WIDTH, cells] = left[rows]
                    rhs[group, i * WIDTH : (i + 1) * WIDTH, cells] = right[rows]

    def multiply(pair, lhs, rhs):
        chunk = plan[pair * 5 + 1]
        for group in range(GROUPS):
            total[chunk, group] += lax.dot_general(
                lhs[group],
                rhs[group],
                (((1,), (1,)), ((), ())),
                preferred_element_type=jnp.float32,
            )

    for pair in range(DEPTH):

        @pl.when(pair < pairs)
        def _(pair=pair):
            start(jnp.int32(pair))

    total[...] = jnp.zeros_like(total)

    @pl.when(pairs > 0)
    def _():
        finish(jnp.int32(0))
        prepare(jnp.int32(0), lhs_a, rhs_a)

        @pl.when(DEPTH < pairs)
        def _():
            start(jnp.int32(DEPTH))

    def step(twice, carry):
        pair = twice * 2 + 1
        finish(pair)
        multiply(pair - 1, lhs_a, rhs_a)
        prepare(pair, lhs_b, rhs_b)

        @pl.when(pair + DEPTH < pairs)
        def _():
            start(pair + DEPTH)

        @pl.when(pair + 1 < pairs)
        def _():
            finish(pair + 1)

        multiply(pair, lhs_b, rhs_b)
        prepare(pair + 1, lhs_a, rhs_a)

        @pl.when(pair + 1 + DEPTH < pairs)
        def _():
            start(pair + 1 + DEPTH)

        return carry

    lax.fori_loop(0, pairs // 2, step, 0)
    for chunk in range(chunks):
        out_refs[chunk][...] = total[chunk].astype(out_refs[chunk].dtype)


def compact(row_of, gate_of):
    chunks, slots = row_of.shape
    length = chunks * slots
    used = row_of >= 0
    order = jnp.arange(slots, dtype=jnp.int32)
    rank = jnp.sum((used[:, :, None] & (order[:, None] < order[None, :])[None]).astype(jnp.int32), 1)
    padded = (jnp.sum(used.astype(jnp.int32), 1) + 1) // 2 * 2
    index = jnp.arange(chunks, dtype=jnp.int32)
    ends = jnp.sum(jnp.where(index[:, None] <= index[None, :], padded[:, None], 0), 0)
    where = (ends - padded)[:, None] + rank
    place = jnp.arange(length + 4, dtype=jnp.int32)
    hit = (used[:, :, None] & (where[:, :, None] == place)).astype(jnp.int32)
    rows = jnp.sum(hit * jnp.maximum(row_of, 0)[:, :, None], (0, 1))
    slot = jnp.sum(hit * order[None, :, None], (0, 1))
    gate = jnp.sum(jnp.where(hit > 0, gate_of[:, :, None], 0.0), (0, 1))
    chunk = jnp.sum((place[None, ::2] >= ends[:, None]).astype(jnp.int32), 0)
    chunk = jnp.minimum(chunk, chunks - 1)
    count = (ends[-1:] // 2 + 1) // 2 * 2
    pairs = jnp.concatenate([chunk[:, None], rows.reshape(-1, 2), slot.reshape(-1, 2)], 1)
    return jnp.concatenate([count, pairs.reshape(-1)]), gate


def weight_grads(plan, gate_of, grads, stash):
    chunks = len(stash)
    place = pl.BlockSpec(memory_space=pl.ANY)
    operand = pltpu.VMEM((GROUPS, 3 * WIDTH, 2 * CELLS), jnp.bfloat16)
    return pl.pallas_call(
        functools.partial(weight_kernel, chunks),
        out_shape=[jax.ShapeDtypeStruct((GROUPS, 3 * WIDTH, 3 * WIDTH), jnp.bfloat16)] * chunks,
        in_specs=[pl.BlockSpec(memory_space=pltpu.SMEM)] * 2 + [place] * (1 + chunks),
        out_specs=[pl.BlockSpec(memory_space=pltpu.VMEM)] * chunks,
        scratch_shapes=[
            pltpu.VMEM((2 * DEPTH, CHANNELS, CELLS), jnp.bfloat16),
            pltpu.VMEM((2 * DEPTH, CHANNELS, CELLS), jnp.bfloat16),
            operand,
            operand,
            operand,
            operand,
            pltpu.VMEM((chunks, GROUPS, 3 * WIDTH, 3 * WIDTH), jnp.float32),
            pltpu.SemaphoreType.DMA((2 * DEPTH, 2)),
        ],
        compiler_params=pltpu.CompilerParams(vmem_limit_bytes=56 << 20),
        cost_estimate=pl.CostEstimate(flops=1, bytes_accessed=1, transcendentals=0),
    )(plan, gate_of, grads, *stash)


def stack_of(first, others):
    return jnp.concatenate([first[None]] + [o[None] for o in others], 0)


def per_device(out_grad, routes, gates, stash, weights):
    x, e = lax.axis_index("rep"), lax.axis_index("ep")
    z, y, c = e // (NY * NC), e // NC % NY, e % NC
    rows, top = routes.shape
    groups = [[zz * NY * NC + r for zz in range(NZ)] for r in range(NY * NC)]
    grads = lax.all_gather(out_grad, "ep", axis=0, tiled=True, axis_index_groups=groups)

    kept = stash.reshape(NZ, NY, NC, 2, CHANNELS, CELLS)
    offsets = [(0, 0), (0, 1), (1, 0), (3, 0), (1, 1), (3, 1), (2, 0), (2, 1)]

    def sent(kept, d, dc):
        part = lax.dynamic_slice(
            kept, (0, (y + d) % NY, c ^ dc, 0, 0, 0), (NZ, 1, 1, 2, CHANNELS, CELLS)
        )
        return part.reshape(NZ * 2, CHANNELS, CELLS)

    first = [sent(kept, d, dc) for d, dc in offsets[2:4]]
    weights, *first = lax.optimization_barrier((weights, *first))
    mixed = weights[0].transpose(0, 3, 1, 2).reshape(9 * WIDTH, CHANNELS)
    mixed = jnp.pad(mixed, ((0, NX * PIECE - 9 * WIDTH), (0, 0)))
    piece = lax.dynamic_slice_in_dim(mixed, x * PIECE, PIECE, 0)
    note = jnp.concatenate(
        [routes.reshape(1, -1).astype(jnp.bfloat16), gates.reshape(1, -1)], 1
    )
    note = jnp.pad(note, ((0, 15), (0, CHANNELS - 2 * rows * top)))
    held = jnp.concatenate([piece, note], 0)
    kept, held, *first = lax.optimization_barrier((kept, held, *first))
    second = [sent(kept, d, dc) for d, dc in offsets[4:6]]
    held, *second = lax.optimization_barrier((held, *second))
    first = [lax.ppermute(part, "ep", ep_perm(0, d, dc)) for part, (d, dc) in zip(first, offsets[2:])]
    experts = [e - y * NC - c + ((y - d) % NY) * NC + (c ^ dc) for d, dc in offsets]
    experts = jnp.stack(experts)

    up = down = held
    from_z = {0: held}
    for d in range(1, NZ // 2 + 1):
        up = lax.ppermute(up, "ep", ep_perm(1, 0, 0))
        from_z[d] = up
        if d < NZ // 2:
            down = lax.ppermute(down, "ep", ep_perm(-1, 0, 0))
            from_z[NZ - d] = down
    held = jnp.stack([from_z[d] for d in range(NZ)])
    notes = held[:, PIECE, : 2 * rows * top].astype(jnp.float32)
    held = held[:, :PIECE]
    held, kept, *first = lax.optimization_barrier((held, kept, *first))
    second = lax.optimization_barrier((held, *second))[1:]
    own, *rest = [sent(kept, d, dc) for d, dc in offsets[:2] + offsets[6:]]
    sends = zip([rest[0], *second, *rest[1:]], offsets[1:2] + offsets[4:])
    rest = [lax.ppermute(part, "ep", ep_perm(0, d, dc)) for part, (d, dc) in sends]
    chunks = [own, rest[0], *first, *rest[1:]]
    held = stack_of(held, [lax.ppermute(held, "ep", ep_perm(0, d, 0)) for d in range(1, NY)])
    held = held.reshape(NY * NZ, PIECE, CHANNELS)
    quarters = [held] + [lax.ppermute(held, "rep", rep_perm(d)) for d in range(1, NX)]
    quarters[2], chunks[4], chunks[5] = lax.optimization_barrier(
        (quarters[2], chunks[4], chunks[5])
    )
    quarters += [lax.ppermute(quarter, "ep", ep_perm(0, 0, 1)) for quarter in quarters]
    held = jnp.concatenate(quarters, 0)
    held = held.reshape(NC * NX * NY * NZ, PIECE, CHANNELS)

    from_z = (z - jnp.arange(NZ, dtype=jnp.int32)) % NZ
    notes = jnp.sum(
        jnp.where((from_z[:, None] == jnp.arange(NZ)[None])[:, :, None], notes[:, None], 0.0), 0
    )
    named = notes[:, : rows * top].astype(jnp.int32)
    gate = notes[:, rows * top :]
    here = experts[:, None, None] == named[None]
    order = jnp.arange(rows * top, dtype=jnp.int32)
    before = (order[:, None] < order[None, :])[None, None] & here[:, :, :, None]
    earlier = jnp.sum(before.astype(jnp.int32), 2)
    chosen = here[:, :, None, :] & (earlier[:, :, None, :] == jnp.arange(2)[None, None, :, None])
    source_row = jnp.arange(NZ, dtype=jnp.int32)[:, None] * rows + (order // top)[None]
    row_of = jnp.max(jnp.where(chosen, source_row[None, :, None, :], -1), 3)
    gate_of = jnp.sum(jnp.where(chosen, gate[None, :, None, :], 0.0), 3)
    row_of, gate_of = row_of.reshape(8, NZ * 2), gate_of.reshape(8, NZ * 2)
    early, late = compact(row_of[:7], gate_of[:7]), compact(row_of[7:], gate_of[7:])
    flat = routes.reshape(-1)
    at_z, at_y, at_c = flat // (NY * NC), flat // NC % NY, flat % NC
    block = ((y - at_y) % NY) * NZ + (z - at_z) % NZ
    quarter = (x - jnp.arange(NX, dtype=jnp.int32)) % NX
    place = ((at_c ^ c)[:, None] * NX + quarter[None]) * (NZ * NY) + block[:, None]
    in_grad = input_grads(
        place.reshape(-1), gates.reshape(-1).astype(jnp.float32), out_grad, held
    )
    in_grad, plan = lax.optimization_barrier((in_grad, early[0]))
    parts = weight_grads(plan, early[1], grads, chunks[:7])
    parts += weight_grads(*late, grads, chunks[7:])

    total = None
    for part, (d, dc) in zip(parts, offsets):
        if d or dc:
            part = lax.ppermute(part, "ep", ep_perm(0, -d, dc))
        part = part.astype(jnp.float32)
        total = part if total is None else total + part
    total = total.astype(jnp.bfloat16)
    summed = total.astype(jnp.float32)
    for d in range(1, NX):
        summed = summed + lax.ppermute(total, "rep", rep_perm(d)).astype(jnp.float32)
    weight_grad = summed.reshape(GROUPS, 3, WIDTH, 3, WIDTH).transpose(1, 3, 0, 2, 4)
    return in_grad, weight_grad.reshape(1, 9, GROUPS, WIDTH, WIDTH)


def solution(mesh):
    return jax.shard_map(
        per_device,
        mesh=mesh,
        in_specs=(
            P(("rep", "ep"), None, None),
            P(("rep", "ep"), None),
            P(("rep", "ep"), None),
            P("rep", "ep", None, None, None, None),
            P("ep", None, None, None, None),
        ),
        out_specs=(P(("rep", "ep"), None, None), P("ep", None, None, None, None)),
        check_vma=False,
    )
```

```python
import functools

import jax
import jax.numpy as jnp
from jax import lax
from jax.experimental import pallas as pl
from jax.experimental.pallas import tpu as pltpu
from jax.sharding import PartitionSpec as P

SIDE = 16
CELLS = 256
GROUPS = 4
WIDTH = 32
CHANNELS = 128
NZ, NY, NC, NX = 8, 4, 2, 4
PIECE = 80
DEPTH = 8
BATCH = 4


def ep_perm(dz, dy, dc):
    pairs = []
    for z in range(NZ):
        for y in range(NY):
            for c in range(NC):
                to = ((z + dz) % NZ, (y + dy) % NY, c ^ dc)
                pairs.append(((z * NY + y) * NC + c, (to[0] * NY + to[1]) * NC + to[2]))
    return pairs


def rep_perm(dx):
    return [(x, (x + dx) % NX) for x in range(NX)]


def shifted(values, row_step, col_step, cell):
    if row_step == 0 and col_step == 0:
        return values
    rolled = pltpu.roll(values, (-(row_step * SIDE + col_step)) % CELLS, 1)
    row, col = cell // SIDE + row_step, cell % SIDE + col_step
    inside = (row >= 0) & (row < SIDE) & (col >= 0) & (col < SIDE)
    return jnp.where(inside, rolled, jnp.zeros_like(rolled))


def input_kernel(place_ref, gate_ref, grad_ref, weight_ref, out_ref, lhs_ref, rhs_ref, stage_ref):
    cell = lax.broadcasted_iota(jnp.int32, (1, CELLS), 1)
    lane_group = lax.broadcasted_iota(jnp.int32, (WIDTH, CHANNELS), 1) // WIDTH
    for j in range(BATCH):
        patch = pl.program_id(0) * BATCH + j
        grad = grad_ref[j]
        for b in (-1, 0, 1):
            by_col = shifted(grad, 0, -b, cell)
            for a in (-1, 0, 1):
                tap = 3 * (a + 1) + (b + 1)
                rhs_ref[j, tap * CHANNELS : (tap + 1) * CHANNELS, :] = shifted(by_col, -a, 0, cell)
        for k in range(2):
            for quarter in range(NX):
                stage_ref[j, k, quarter * PIECE : (quarter + 1) * PIECE, :] = weight_ref[
                    place_ref[(patch * 2 + k) * NX + quarter]
                ]
            for tap in range(9):
                kernel = stage_ref[j, k, tap * WIDTH : (tap + 1) * WIDTH, :]
                for group in range(GROUPS):
                    row = k * CHANNELS + group * WIDTH
                    lhs_ref[
                        j, row : row + WIDTH, tap * CHANNELS : (tap + 1) * CHANNELS
                    ] = jnp.where(lane_group == group, kernel, jnp.zeros_like(kernel))
        both = jnp.dot(lhs_ref[j], rhs_ref[j], preferred_element_type=jnp.float32)
        total = (
            gate_ref[patch * 2] * both[:CHANNELS] + gate_ref[patch * 2 + 1] * both[CHANNELS:]
        )
        out_ref[j] = total.astype(jnp.bfloat16)


def input_grads(place, gate, grad, weight):
    count = grad.shape[0]
    return pl.pallas_call(
        input_kernel,
        out_shape=jax.ShapeDtypeStruct(grad.shape, jnp.bfloat16),
        grid=(count // BATCH,),
        in_specs=[
            pl.BlockSpec(memory_space=pltpu.SMEM),
            pl.BlockSpec(memory_space=pltpu.SMEM),
            pl.BlockSpec((BATCH, CHANNELS, CELLS), lambda i: (i, 0, 0)),
            pl.BlockSpec(memory_space=pltpu.VMEM),
        ],
        out_specs=pl.BlockSpec((BATCH, CHANNELS, CELLS), lambda i: (i, 0, 0)),
        scratch_shapes=[
            pltpu.VMEM((BATCH, 2 * CHANNELS, 9 * CHANNELS), jnp.bfloat16),
            pltpu.VMEM((BATCH, 9 * CHANNELS, CELLS), jnp.bfloat16),
            pltpu.VMEM((BATCH, 2, NX * PIECE, CHANNELS), jnp.bfloat16),
        ],
        compiler_params=pltpu.CompilerParams(vmem_limit_bytes=28 << 20),
        cost_estimate=pl.CostEstimate(flops=1, bytes_accessed=1, transcendentals=0),
    )(place, gate, grad, weight)


def weight_kernel(chunks, plan, gate_of, grads, *refs):
    stash, out_refs, refs = refs[:chunks], refs[chunks : 2 * chunks], refs[2 * chunks :]
    grad_buf, stash_buf, lhs_a, rhs_a, lhs_b, rhs_b, total, sems = refs
    cell = lax.broadcasted_iota(jnp.int32, (1, CELLS), 1)
    pairs = plan[0]

    def start(pair):
        for j in range(2):
            slot = (pair % DEPTH) * 2 + j
            pltpu.make_async_copy(
                grads.at[plan[pair * 5 + 2 + j]], grad_buf.at[slot], sems.at[slot, 0]
            ).start()
        for chunk in range(chunks):

            @pl.when(plan[pair * 5 + 1] == chunk)
            def _(chunk=chunk):
                for j in range(2):
                    slot = (pair % DEPTH) * 2 + j
                    pltpu.make_async_copy(
                        stash[chunk].at[plan[pair * 5 + 4 + j]], stash_buf.at[slot], sems.at[slot, 1]
                    ).start()

    def finish(pair):
        for j in range(2):
            slot = (pair % DEPTH) * 2 + j
            pltpu.make_async_copy(grads.at[0], grad_buf.at[slot], sems.at[slot, 0]).wait()
            pltpu.make_async_copy(stash[0].at[0], stash_buf.at[slot], sems.at[slot, 1]).wait()

    def prepare(pair, lhs, rhs):
        for j in range(2):
            slot = (pair % DEPTH) * 2 + j
            cells = slice(j * CELLS, (j + 1) * CELLS)
            grad = grad_buf[slot].astype(jnp.float32) * gate_of[pair * 2 + j]
            grad = grad.astype(jnp.bfloat16)
            kept = stash_buf[slot]
            for i, step_by in enumerate((-1, 0, 1)):
                left = shifted(grad, -step_by, 0, cell)
                right = shifted(kept, 0, step_by, cell)
                for group in range(GROUPS):
                    rows = slice(group * WIDTH, (group + 1) * WIDTH)
                    lhs[group, i * WIDTH : (i + 1) * WIDTH, cells] = left[rows]
                    rhs[group, i * WIDTH : (i + 1) * WIDTH, cells] = right[rows]

    def multiply(pair, lhs, rhs):
        chunk = plan[pair * 5 + 1]
        for group in range(GROUPS):
            total[chunk, group] += lax.dot_general(
                lhs[group],
                rhs[group],
                (((1,), (1,)), ((), ())),
                preferred_element_type=jnp.float32,
            )

    for pair in range(DEPTH):

        @pl.when(pair < pairs)
        def _(pair=pair):
            start(jnp.int32(pair))

    total[...] = jnp.zeros_like(total)

    @pl.when(pairs > 0)
    def _():
        finish(jnp.int32(0))
        prepare(jnp.int32(0), lhs_a, rhs_a)

        @pl.when(DEPTH < pairs)
        def _():
            start(jnp.int32(DEPTH))

    def step(twice, carry):
        pair = twice * 2 + 1
        finish(pair)
        multiply(pair - 1, lhs_a, rhs_a)
        prepare(pair, lhs_b, rhs_b)

        @pl.when(pair + DEPTH < pairs)
        def _():
            start(pair + DEPTH)

        @pl.when(pair + 1 < pairs)
        def _():
            finish(pair + 1)

        multiply(pair, lhs_b, rhs_b)
        prepare(pair + 1, lhs_a, rhs_a)

        @pl.when(pair + 1 + DEPTH < pairs)
        def _():
            start(pair + 1 + DEPTH)

        return carry

    lax.fori_loop(0, pairs // 2, step, 0)
    for chunk in range(chunks):
        out_refs[chunk][...] = total[chunk].astype(out_refs[chunk].dtype)


def compact(row_of, gate_of):
    chunks, slots = row_of.shape
    length = chunks * slots
    used = row_of >= 0
    order = jnp.arange(slots, dtype=jnp.int32)
    rank = jnp.sum((used[:, :, None] & (order[:, None] < order[None, :])[None]).astype(jnp.int32), 1)
    padded = (jnp.sum(used.astype(jnp.int32), 1) + 1) // 2 * 2
    index = jnp.arange(chunks, dtype=jnp.int32)
    ends = jnp.sum(jnp.where(index[:, None] <= index[None, :], padded[:, None], 0), 0)
    where = (ends - padded)[:, None] + rank
    place = jnp.arange(length + 4, dtype=jnp.int32)
    hit = (used[:, :, None] & (where[:, :, None] == place)).astype(jnp.int32)
    rows = jnp.sum(hit * jnp.maximum(row_of, 0)[:, :, None], (0, 1))
    slot = jnp.sum(hit * order[None, :, None], (0, 1))
    gate = jnp.sum(jnp.where(hit > 0, gate_of[:, :, None], 0.0), (0, 1))
    chunk = jnp.sum((place[None, ::2] >= ends[:, None]).astype(jnp.int32), 0)
    chunk = jnp.minimum(chunk, chunks - 1)
    count = (ends[-1:] // 2 + 1) // 2 * 2
    pairs = jnp.concatenate([chunk[:, None], rows.reshape(-1, 2), slot.reshape(-1, 2)], 1)
    return jnp.concatenate([count, pairs.reshape(-1)]), gate


def weight_grads(plan, gate_of, grads, stash):
    chunks = len(stash)
    place = pl.BlockSpec(memory_space=pl.ANY)
    operand = pltpu.VMEM((GROUPS, 3 * WIDTH, 2 * CELLS), jnp.bfloat16)
    return pl.pallas_call(
        functools.partial(weight_kernel, chunks),
        out_shape=[jax.ShapeDtypeStruct((GROUPS, 3 * WIDTH, 3 * WIDTH), jnp.bfloat16)] * chunks,
        in_specs=[pl.BlockSpec(memory_space=pltpu.SMEM)] * 2 + [place] * (1 + chunks),
        out_specs=[pl.BlockSpec(memory_space=pltpu.VMEM)] * chunks,
        scratch_shapes=[
            pltpu.VMEM((2 * DEPTH, CHANNELS, CELLS), jnp.bfloat16),
            pltpu.VMEM((2 * DEPTH, CHANNELS, CELLS), jnp.bfloat16),
            operand,
            operand,
            operand,
            operand,
            pltpu.VMEM((chunks, GROUPS, 3 * WIDTH, 3 * WIDTH), jnp.float32),
            pltpu.SemaphoreType.DMA((2 * DEPTH, 2)),
        ],
        compiler_params=pltpu.CompilerParams(vmem_limit_bytes=56 << 20),
        cost_estimate=pl.CostEstimate(flops=1, bytes_accessed=1, transcendentals=0),
    )(plan, gate_of, grads, *stash)


def stack_of(first, others):
    return jnp.concatenate([first[None]] + [o[None] for o in others], 0)


def per_device(out_grad, routes, gates, stash, weights):
    x, e = lax.axis_index("rep"), lax.axis_index("ep")
    z, y, c = e // (NY * NC), e // NC % NY, e % NC
    rows, top = routes.shape
    groups = [[zz * NY * NC + r for zz in range(NZ)] for r in range(NY * NC)]
    grads = lax.all_gather(out_grad, "ep", axis=0, tiled=True, axis_index_groups=groups)

    kept = stash.reshape(NZ, NY, NC, 2, CHANNELS, CELLS)
    offsets = [(0, 0), (0, 1), (1, 0), (3, 0), (1, 1), (3, 1), (2, 0), (2, 1)]

    def sent(kept, d, dc):
        part = lax.dynamic_slice(
            kept, (0, (y + d) % NY, c ^ dc, 0, 0, 0), (NZ, 1, 1, 2, CHANNELS, CELLS)
        )
        return part.reshape(NZ * 2, CHANNELS, CELLS)

    first = [sent(kept, d, dc) for d, dc in offsets[2:4]]
    weights, *first = lax.optimization_barrier((weights, *first))
    mixed = weights[0].transpose(0, 3, 1, 2).reshape(9 * WIDTH, CHANNELS)
    mixed = jnp.pad(mixed, ((0, NX * PIECE - 9 * WIDTH), (0, 0)))
    piece = lax.dynamic_slice_in_dim(mixed, x * PIECE, PIECE, 0)
    note = jnp.concatenate(
        [routes.reshape(1, -1).astype(jnp.bfloat16), gates.reshape(1, -1)], 1
    )
    note = jnp.pad(note, ((0, 15), (0, CHANNELS - 2 * rows * top)))
    held = jnp.concatenate([piece, note], 0)
    kept, held, *first = lax.optimization_barrier((kept, held, *first))
    own, *rest = [sent(kept, d, dc) for d, dc in offsets[:2] + offsets[4:]]
    experts = [e - y * NC - c + ((y - d) % NY) * NC + (c ^ dc) for d, dc in offsets]
    experts = jnp.stack(experts)

    up = down = held
    from_z = {0: held}
    for d in range(1, NZ // 2 + 1):
        up = lax.ppermute(up, "ep", ep_perm(1, 0, 0))
        from_z[d] = up
        if d < NZ // 2:
            down = lax.ppermute(down, "ep", ep_perm(-1, 0, 0))
            from_z[NZ - d] = down
    held = jnp.stack([from_z[d] for d in range(NZ)])
    notes = held[:, PIECE, : 2 * rows * top].astype(jnp.float32)
    held = held[:, :PIECE]
    held, *rest = lax.optimization_barrier((held, *rest))
    rest = rest[:1] + first + rest[1:]
    chunks = [own] + [
        lax.ppermute(part, "ep", ep_perm(0, d, dc)) for part, (d, dc) in zip(rest, offsets[1:])
    ]
    held = stack_of(held, [lax.ppermute(held, "ep", ep_perm(0, d, 0)) for d in range(1, NY)])
    held = held.reshape(NY * NZ, PIECE, CHANNELS)
    held, chunks[2], chunks[3] = lax.optimization_barrier((held, chunks[2], chunks[3]))
    quarters = [held] + [lax.ppermute(held, "rep", rep_perm(d)) for d in range(1, NX)]
    quarters[2], chunks[4], chunks[5] = lax.optimization_barrier(
        (quarters[2], chunks[4], chunks[5])
    )
    quarters += [lax.ppermute(quarter, "ep", ep_perm(0, 0, 1)) for quarter in quarters]
    held = jnp.concatenate(quarters, 0)
    held, chunks[6] = lax.optimization_barrier((held, chunks[6]))
    held = held.reshape(NC * NX * NY * NZ, PIECE, CHANNELS)

    from_z = (z - jnp.arange(NZ, dtype=jnp.int32)) % NZ
    notes = jnp.sum(
        jnp.where((from_z[:, None] == jnp.arange(NZ)[None])[:, :, None], notes[:, None], 0.0), 0
    )
    named = notes[:, : rows * top].astype(jnp.int32)
    gate = notes[:, rows * top :]
    here = experts[:, None, None] == named[None]
    order = jnp.arange(rows * top, dtype=jnp.int32)
    before = (order[:, None] < order[None, :])[None, None] & here[:, :, :, None]
    earlier = jnp.sum(before.astype(jnp.int32), 2)
    chosen = here[:, :, None, :] & (earlier[:, :, None, :] == jnp.arange(2)[None, None, :, None])
    source_row = jnp.arange(NZ, dtype=jnp.int32)[:, None] * rows + (order // top)[None]
    row_of = jnp.max(jnp.where(chosen, source_row[None, :, None, :], -1), 3)
    gate_of = jnp.sum(jnp.where(chosen, gate[None, :, None, :], 0.0), 3)
    row_of, gate_of = row_of.reshape(8, NZ * 2), gate_of.reshape(8, NZ * 2)
    early, late = compact(row_of[:7], gate_of[:7]), compact(row_of[7:], gate_of[7:])
    flat = routes.reshape(-1)
    at_z, at_y, at_c = flat // (NY * NC), flat // NC % NY, flat % NC
    block = ((y - at_y) % NY) * NZ + (z - at_z) % NZ
    quarter = (x - jnp.arange(NX, dtype=jnp.int32)) % NX
    place = ((at_c ^ c)[:, None] * NX + quarter[None]) * (NZ * NY) + block[:, None]
    in_grad = input_grads(
        place.reshape(-1), gates.reshape(-1).astype(jnp.float32), out_grad, held
    )
    in_grad, plan = lax.optimization_barrier((in_grad, early[0]))
    parts = weight_grads(plan, early[1], grads, chunks[:7])
    parts += weight_grads(*late, grads, chunks[7:])

    total = None
    for part, (d, dc) in zip(parts, offsets):
        if d or dc:
            part = lax.ppermute(part, "ep", ep_perm(0, -d, dc))
        part = part.astype(jnp.float32)
        total = part if total is None else total + part
    total = total.astype(jnp.bfloat16)
    summed = total.astype(jnp.float32)
    for d in range(1, NX):
        summed = summed + lax.ppermute(total, "rep", rep_perm(d)).astype(jnp.float32)
    weight_grad = summed.reshape(GROUPS, 3, WIDTH, 3, WIDTH).transpose(1, 3, 0, 2, 4)
    return in_grad, weight_grad.reshape(1, 9, GROUPS, WIDTH, WIDTH)


def solution(mesh):
    return jax.shard_map(
        per_device,
        mesh=mesh,
        in_specs=(
            P(("rep", "ep"), None, None),
            P(("rep", "ep"), None),
            P(("rep", "ep"), None),
            P("rep", "ep", None, None, None, None),
            P("ep", None, None, None, None),
        ),
        out_specs=(P(("rep", "ep"), None, None), P("ep", None, None, None, None)),
        check_vma=False,
    )
```

```python
import functools

import jax
import jax.numpy as jnp
from jax import lax
from jax.experimental import pallas as pl
from jax.experimental.pallas import tpu as pltpu
from jax.sharding import PartitionSpec as P

SIDE = 16
CELLS = 256
GROUPS = 4
WIDTH = 32
CHANNELS = 128
NZ, NY, NC, NX = 8, 4, 2, 4
PIECE = 80
DEPTH = 8
BATCH = 4


def ep_perm(dz, dy, dc):
    pairs = []
    for z in range(NZ):
        for y in range(NY):
            for c in range(NC):
                to = ((z + dz) % NZ, (y + dy) % NY, c ^ dc)
                pairs.append(((z * NY + y) * NC + c, (to[0] * NY + to[1]) * NC + to[2]))
    return pairs


def rep_perm(dx):
    return [(x, (x + dx) % NX) for x in range(NX)]


def shifted(values, row_step, col_step, cell):
    if row_step == 0 and col_step == 0:
        return values
    rolled = pltpu.roll(values, (-(row_step * SIDE + col_step)) % CELLS, 1)
    row, col = cell // SIDE + row_step, cell % SIDE + col_step
    inside = (row >= 0) & (row < SIDE) & (col >= 0) & (col < SIDE)
    return jnp.where(inside, rolled, jnp.zeros_like(rolled))


def input_kernel(place_ref, gate_ref, grad_ref, weight_ref, out_ref, lhs_ref, rhs_ref, stage_ref):
    cell = lax.broadcasted_iota(jnp.int32, (1, CELLS), 1)
    lane_group = lax.broadcasted_iota(jnp.int32, (WIDTH, CHANNELS), 1) // WIDTH
    for j in range(BATCH):
        patch = pl.program_id(0) * BATCH + j
        grad = grad_ref[j]
        for b in (-1, 0, 1):
            by_col = shifted(grad, 0, -b, cell)
            for a in (-1, 0, 1):
                tap = 3 * (a + 1) + (b + 1)
                rhs_ref[j, tap * CHANNELS : (tap + 1) * CHANNELS, :] = shifted(by_col, -a, 0, cell)
        for k in range(2):
            for quarter in range(NX):
                stage_ref[j, k, quarter * PIECE : (quarter + 1) * PIECE, :] = weight_ref[
                    place_ref[(patch * 2 + k) * NX + quarter]
                ]
            for tap in range(9):
                kernel = stage_ref[j, k, tap * WIDTH : (tap + 1) * WIDTH, :]
                for group in range(GROUPS):
                    row = k * CHANNELS + group * WIDTH
                    lhs_ref[
                        j, row : row + WIDTH, tap * CHANNELS : (tap + 1) * CHANNELS
                    ] = jnp.where(lane_group == group, kernel, jnp.zeros_like(kernel))
        both = jnp.dot(lhs_ref[j], rhs_ref[j], preferred_element_type=jnp.float32)
        total = (
            gate_ref[patch * 2] * both[:CHANNELS] + gate_ref[patch * 2 + 1] * both[CHANNELS:]
        )
        out_ref[j] = total.astype(jnp.bfloat16)


def input_grads(place, gate, grad, weight):
    count = grad.shape[0]
    return pl.pallas_call(
        input_kernel,
        out_shape=jax.ShapeDtypeStruct(grad.shape, jnp.bfloat16),
        grid=(count // BATCH,),
        in_specs=[
            pl.BlockSpec(memory_space=pltpu.SMEM),
            pl.BlockSpec(memory_space=pltpu.SMEM),
            pl.BlockSpec((BATCH, CHANNELS, CELLS), lambda i: (i, 0, 0)),
            pl.BlockSpec(memory_space=pltpu.VMEM),
        ],
        out_specs=pl.BlockSpec((BATCH, CHANNELS, CELLS), lambda i: (i, 0, 0)),
        scratch_shapes=[
            pltpu.VMEM((BATCH, 2 * CHANNELS, 9 * CHANNELS), jnp.bfloat16),
            pltpu.VMEM((BATCH, 9 * CHANNELS, CELLS), jnp.bfloat16),
            pltpu.VMEM((BATCH, 2, NX * PIECE, CHANNELS), jnp.bfloat16),
        ],
        compiler_params=pltpu.CompilerParams(vmem_limit_bytes=28 << 20),
        cost_estimate=pl.CostEstimate(flops=1, bytes_accessed=1, transcendentals=0),
    )(place, gate, grad, weight)


def weight_kernel(chunks, plan, gate_of, grads, *refs):
    stash, out_refs, refs = refs[:chunks], refs[chunks : 2 * chunks], refs[2 * chunks :]
    grad_buf, stash_buf, lhs_a, rhs_a, lhs_b, rhs_b, total, sems = refs
    cell = lax.broadcasted_iota(jnp.int32, (1, CELLS), 1)
    pairs = plan[0]

    def start(pair):
        for j in range(2):
            slot = (pair % DEPTH) * 2 + j
            pltpu.make_async_copy(
                grads.at[plan[pair * 5 + 2 + j]], grad_buf.at[slot], sems.at[slot, 0]
            ).start()
        for chunk in range(chunks):

            @pl.when(plan[pair * 5 + 1] == chunk)
            def _(chunk=chunk):
                for j in range(2):
                    slot = (pair % DEPTH) * 2 + j
                    pltpu.make_async_copy(
                        stash[chunk].at[plan[pair * 5 + 4 + j]], stash_buf.at[slot], sems.at[slot, 1]
                    ).start()

    def finish(pair):
        for j in range(2):
            slot = (pair % DEPTH) * 2 + j
            pltpu.make_async_copy(grads.at[0], grad_buf.at[slot], sems.at[slot, 0]).wait()
            pltpu.make_async_copy(stash[0].at[0], stash_buf.at[slot], sems.at[slot, 1]).wait()

    def prepare(pair, lhs, rhs):
        for j in range(2):
            slot = (pair % DEPTH) * 2 + j
            cells = slice(j * CELLS, (j + 1) * CELLS)
            grad = grad_buf[slot].astype(jnp.float32) * gate_of[pair * 2 + j]
            grad = grad.astype(jnp.bfloat16)
            kept = stash_buf[slot]
            for i, step_by in enumerate((-1, 0, 1)):
                left = shifted(grad, -step_by, 0, cell)
                right = shifted(kept, 0, step_by, cell)
                for group in range(GROUPS):
                    rows = slice(group * WIDTH, (group + 1) * WIDTH)
                    lhs[group, i * WIDTH : (i + 1) * WIDTH, cells] = left[rows]
                    rhs[group, i * WIDTH : (i + 1) * WIDTH, cells] = right[rows]

    def multiply(pair, lhs, rhs):
        chunk = plan[pair * 5 + 1]
        for group in range(GROUPS):
            total[chunk, group] += lax.dot_general(
                lhs[group],
                rhs[group],
                (((1,), (1,)), ((), ())),
                preferred_element_type=jnp.float32,
            )

    for pair in range(DEPTH):

        @pl.when(pair < pairs)
        def _(pair=pair):
            start(jnp.int32(pair))

    total[...] = jnp.zeros_like(total)

    @pl.when(pairs > 0)
    def _():
        finish(jnp.int32(0))
        prepare(jnp.int32(0), lhs_a, rhs_a)

        @pl.when(DEPTH < pairs)
        def _():
            start(jnp.int32(DEPTH))

    def step(twice, carry):
        pair = twice * 2 + 1
        finish(pair)
        multiply(pair - 1, lhs_a, rhs_a)
        prepare(pair, lhs_b, rhs_b)

        @pl.when(pair + DEPTH < pairs)
        def _():
            start(pair + DEPTH)

        @pl.when(pair + 1 < pairs)
        def _():
            finish(pair + 1)

        multiply(pair, lhs_b, rhs_b)
        prepare(pair + 1, lhs_a, rhs_a)

        @pl.when(pair + 1 + DEPTH < pairs)
        def _():
            start(pair + 1 + DEPTH)

        return carry

    lax.fori_loop(0, pairs // 2, step, 0)
    for chunk in range(chunks):
        out_refs[chunk][...] = total[chunk].astype(out_refs[chunk].dtype)


def compact(row_of, gate_of):
    chunks, slots = row_of.shape
    length = chunks * slots
    used = row_of >= 0
    order = jnp.arange(slots, dtype=jnp.int32)
    rank = jnp.sum((used[:, :, None] & (order[:, None] < order[None, :])[None]).astype(jnp.int32), 1)
    padded = (jnp.sum(used.astype(jnp.int32), 1) + 1) // 2 * 2
    index = jnp.arange(chunks, dtype=jnp.int32)
    ends = jnp.sum(jnp.where(index[:, None] <= index[None, :], padded[:, None], 0), 0)
    where = (ends - padded)[:, None] + rank
    place = jnp.arange(length + 4, dtype=jnp.int32)
    hit = (used[:, :, None] & (where[:, :, None] == place)).astype(jnp.int32)
    rows = jnp.sum(hit * jnp.maximum(row_of, 0)[:, :, None], (0, 1))
    slot = jnp.sum(hit * order[None, :, None], (0, 1))
    gate = jnp.sum(jnp.where(hit > 0, gate_of[:, :, None], 0.0), (0, 1))
    chunk = jnp.sum((place[None, ::2] >= ends[:, None]).astype(jnp.int32), 0)
    chunk = jnp.minimum(chunk, chunks - 1)
    count = (ends[-1:] // 2 + 1) // 2 * 2
    pairs = jnp.concatenate([chunk[:, None], rows.reshape(-1, 2), slot.reshape(-1, 2)], 1)
    return jnp.concatenate([count, pairs.reshape(-1)]), gate


def weight_grads(plan, gate_of, grads, stash):
    chunks = len(stash)
    place = pl.BlockSpec(memory_space=pl.ANY)
    operand = pltpu.VMEM((GROUPS, 3 * WIDTH, 2 * CELLS), jnp.bfloat16)
    return pl.pallas_call(
        functools.partial(weight_kernel, chunks),
        out_shape=[jax.ShapeDtypeStruct((GROUPS, 3 * WIDTH, 3 * WIDTH), jnp.bfloat16)] * chunks,
        in_specs=[pl.BlockSpec(memory_space=pltpu.SMEM)] * 2 + [place] * (1 + chunks),
        out_specs=[pl.BlockSpec(memory_space=pltpu.VMEM)] * chunks,
        scratch_shapes=[
            pltpu.VMEM((2 * DEPTH, CHANNELS, CELLS), jnp.bfloat16),
            pltpu.VMEM((2 * DEPTH, CHANNELS, CELLS), jnp.bfloat16),
            operand,
            operand,
            operand,
            operand,
            pltpu.VMEM((chunks, GROUPS, 3 * WIDTH, 3 * WIDTH), jnp.float32),
            pltpu.SemaphoreType.DMA((2 * DEPTH, 2)),
        ],
        compiler_params=pltpu.CompilerParams(vmem_limit_bytes=56 << 20),
        cost_estimate=pl.CostEstimate(flops=1, bytes_accessed=1, transcendentals=0),
    )(plan, gate_of, grads, *stash)


def stack_of(first, others):
    return jnp.concatenate([first[None]] + [o[None] for o in others], 0)


def per_device(out_grad, routes, gates, stash, weights):
    x, e = lax.axis_index("rep"), lax.axis_index("ep")
    z, y, c = e // (NY * NC), e // NC % NY, e % NC
    rows, top = routes.shape
    groups = [[zz * NY * NC + r for zz in range(NZ)] for r in range(NY * NC)]
    grads = lax.all_gather(out_grad, "ep", axis=0, tiled=True, axis_index_groups=groups)

    kept = stash.reshape(NZ, NY, NC, 2, CHANNELS, CELLS)
    offsets = [(0, 0), (0, 1), (1, 0), (3, 0), (1, 1), (3, 1), (2, 0), (2, 1)]

    def sent(kept, d, dc):
        part = lax.dynamic_slice(
            kept, (0, (y + d) % NY, c ^ dc, 0, 0, 0), (NZ, 1, 1, 2, CHANNELS, CELLS)
        )
        return part.reshape(NZ * 2, CHANNELS, CELLS)

    first = [sent(kept, d, dc) for d, dc in offsets[2:4]]
    weights, *first = lax.optimization_barrier((weights, *first))
    mixed = weights[0].transpose(0, 3, 1, 2).reshape(9 * WIDTH, CHANNELS)
    mixed = jnp.pad(mixed, ((0, NX * PIECE - 9 * WIDTH), (0, 0)))
    piece = lax.dynamic_slice_in_dim(mixed, x * PIECE, PIECE, 0)
    note = jnp.concatenate(
        [routes.reshape(1, -1).astype(jnp.bfloat16), gates.reshape(1, -1)], 1
    )
    note = jnp.pad(note, ((0, 15), (0, CHANNELS - 2 * rows * top)))
    held = jnp.concatenate([piece, note], 0)
    kept, held, *first = lax.optimization_barrier((kept, held, *first))
    own, *rest = [sent(kept, d, dc) for d, dc in offsets[:2] + offsets[4:]]
    experts = [e - y * NC - c + ((y - d) % NY) * NC + (c ^ dc) for d, dc in offsets]
    experts = jnp.stack(experts)

    up = down = held
    from_z = {0: held}
    for d in range(1, NZ // 2 + 1):
        up = lax.ppermute(up, "ep", ep_perm(1, 0, 0))
        from_z[d] = up
        if d < NZ // 2:
            down = lax.ppermute(down, "ep", ep_perm(-1, 0, 0))
            from_z[NZ - d] = down
    held = jnp.stack([from_z[d] for d in range(NZ)])
    notes = held[:, PIECE, : 2 * rows * top].astype(jnp.float32)
    held = held[:, :PIECE]
    held, *rest = lax.optimization_barrier((held, *rest))
    rest = rest[:1] + first + rest[1:]
    chunks = [own] + [
        lax.ppermute(part, "ep", ep_perm(0, d, dc)) for part, (d, dc) in zip(rest, offsets[1:])
    ]
    held = stack_of(held, [lax.ppermute(held, "ep", ep_perm(0, d, 0)) for d in range(1, NY)])
    held = held.reshape(NY * NZ, PIECE, CHANNELS)
    held, chunks[2], chunks[3] = lax.optimization_barrier((held, chunks[2], chunks[3]))
    quarters = [held] + [lax.ppermute(held, "rep", rep_perm(d)) for d in range(1, NX)]
    quarters[1], chunks[4], chunks[5] = lax.optimization_barrier(
        (quarters[1], chunks[4], chunks[5])
    )
    quarters += [lax.ppermute(quarter, "ep", ep_perm(0, 0, 1)) for quarter in quarters]
    held = jnp.concatenate(quarters, 0)
    held, chunks[6] = lax.optimization_barrier((held, chunks[6]))
    held = held.reshape(NC * NX * NY * NZ, PIECE, CHANNELS)

    from_z = (z - jnp.arange(NZ, dtype=jnp.int32)) % NZ
    notes = jnp.sum(
        jnp.where((from_z[:, None] == jnp.arange(NZ)[None])[:, :, None], notes[:, None], 0.0), 0
    )
    named = notes[:, : rows * top].astype(jnp.int32)
    gate = notes[:, rows * top :]
    here = experts[:, None, None] == named[None]
    order = jnp.arange(rows * top, dtype=jnp.int32)
    before = (order[:, None] < order[None, :])[None, None] & here[:, :, :, None]
    earlier = jnp.sum(before.astype(jnp.int32), 2)
    chosen = here[:, :, None, :] & (earlier[:, :, None, :] == jnp.arange(2)[None, None, :, None])
    source_row = jnp.arange(NZ, dtype=jnp.int32)[:, None] * rows + (order // top)[None]
    row_of = jnp.max(jnp.where(chosen, source_row[None, :, None, :], -1), 3)
    gate_of = jnp.sum(jnp.where(chosen, gate[None, :, None, :], 0.0), 3)
    row_of, gate_of = row_of.reshape(8, NZ * 2), gate_of.reshape(8, NZ * 2)
    early, late = compact(row_of[:7], gate_of[:7]), compact(row_of[7:], gate_of[7:])
    flat = routes.reshape(-1)
    at_z, at_y, at_c = flat // (NY * NC), flat // NC % NY, flat % NC
    block = ((y - at_y) % NY) * NZ + (z - at_z) % NZ
    quarter = (x - jnp.arange(NX, dtype=jnp.int32)) % NX
    place = ((at_c ^ c)[:, None] * NX + quarter[None]) * (NZ * NY) + block[:, None]
    in_grad = input_grads(
        place.reshape(-1), gates.reshape(-1).astype(jnp.float32), out_grad, held
    )
    in_grad, plan = lax.optimization_barrier((in_grad, early[0]))
    parts = weight_grads(plan, early[1], grads, chunks[:7])
    parts += weight_grads(*late, grads, chunks[7:])

    total = None
    for part, (d, dc) in zip(parts, offsets):
        if d or dc:
            part = lax.ppermute(part, "ep", ep_perm(0, -d, dc))
        part = part.astype(jnp.float32)
        total = part if total is None else total + part
    total = total.astype(jnp.bfloat16)
    summed = total.astype(jnp.float32)
    for d in range(1, NX):
        summed = summed + lax.ppermute(total, "rep", rep_perm(d)).astype(jnp.float32)
    weight_grad = summed.reshape(GROUPS, 3, WIDTH, 3, WIDTH).transpose(1, 3, 0, 2, 4)
    return in_grad, weight_grad.reshape(1, 9, GROUPS, WIDTH, WIDTH)


def solution(mesh):
    return jax.shard_map(
        per_device,
        mesh=mesh,
        in_specs=(
            P(("rep", "ep"), None, None),
            P(("rep", "ep"), None),
            P(("rep", "ep"), None),
            P("rep", "ep", None, None, None, None),
            P("ep", None, None, None, None),
        ),
        out_specs=(P(("rep", "ep"), None, None), P("ep", None, None, None, None)),
        check_vma=False,
    )
```
